128 devices in a mesh: grp: 8 (over y, core), tp: 16 (over x, z).
Axes of the slice: x: 4, y: 4, z: 4, core: 2. Of those that a mesh axis runs over, the one named last changes fastest.
Arguments:
- embedded: bfloat16 [2, 4096, 8192], P(None, 'grp', 'tp'), may hold values from -6 to 6
- norm_gain: float32 [8192], replicated, may hold values from 0.25 to 1.75
- w_query: bfloat16 [8192, 8192], P(None, 'tp'), may hold values from -0.0625 to 0.0625
- w_keyval: bfloat16 [8192, 2048], P(None, 'tp'), may hold values from -0.0625 to 0.0625
- w_out: bfloat16 [8192, 8192], P('tp'), may hold values from -0.75 to 0.75
- prefix_kv: bfloat16 [64, 512, 2048], P('grp', None, 'tp'), may hold values from -3000 to 3000
- prefix_len: int32 [64], replicated, may hold values from 64 to 512, as said below
- needed: int32 [8, 16], replicated, may hold values from 0 to 63, as said below
- row_slot: int32 [8, 512], P('grp'), may hold values from 0 to 15, never falling along the last dimension, each value on 1 to 64 neighbouring positions
Outputs:
- mixed: bfloat16 [2, 4096, 8192], P(None, 'grp', 'tp')
The draws below stay inside these ranges and needn't reach their ends.
Inputs may be any that keep to these rules, and one draw needn't show every extreme that they name: `needed`: prefix p belongs to group p // 8. Each group lists 16 different prefixes; from one owner group it lists at most 2 prefixes p with p % 8 < 4 and at most 2 others, and in every group some owner group gives exactly 2 of each. `prefix_len`: prefix p has more than 256 tokens exactly when p % 8 < 4. Some prefix has exactly 512 tokens. `row_slot`: within each group the rows are sorted by slot; every slot has 1 to 64 rows, exactly 64 in some slot.
All inputs are finite; a program needn't handle non-finite values.
Results may differ from the reference program's by a relative error of at most 0.02.
Values may be sent and summed in bfloat16 or wider, within the bound.
A program may use at most 128 MiB of HBM per device.

```python
import math
import jax
import jax.numpy as jnp
import numpy as np
from jax import lax

D = 8192
H = 64
KVH = 8
HEAD = 128
ROWS = 512
STEPS = 2
NEED = 16
PREF = 8
CAP = 4
LEN = 512
MOST = 64
SPLIT = 2
HALF = 64
NPRE = 64
TOTAL_ROWS = 4096
N_GRP = 8


def draw_prefix_len(key, part):
    key = jax.random.fold_in(key, 21)
    long_key, short_key, group_key, place_key = jax.random.split(key, 4)
    local = jnp.arange(NPRE) % PREF
    is_long = local < PREF // 2
    long_lengths = jax.random.randint(long_key, (NPRE,), LEN // 2 + 1, LEN + 1)
    short_lengths = jax.random.randint(short_key, (NPRE,), LEN // 8, LEN // 2 + 1)
    lengths = jnp.where(is_long, long_lengths, short_lengths)
    longest = jax.random.randint(group_key, (), 0, N_GRP) * PREF + jax.random.randint(place_key, (), 0, PREF // 2)
    return jnp.where(jnp.arange(NPRE) == longest, LEN, lengths).astype(jnp.int32)


def draw_needed(key, part):
    key = jax.random.fold_in(key, 37)
    long_key, short_key, favour_key, score_key = jax.random.split(key, 4)
    half_pref = PREF // 2
    half_cap = CAP // 2
    long_order = jax.random.randint(long_key, (N_GRP, N_GRP, half_pref), 0, 1 << 16) * half_pref + jnp.arange(half_pref)[None, None, :]
    short_order = jax.random.randint(short_key, (N_GRP, N_GRP, half_pref), 0, 1 << 16) * half_pref + jnp.arange(half_pref)[None, None, :]
    long_chosen = jnp.argsort(long_order, axis=-1, stable=True)[:, :, :half_cap]
    short_chosen = jnp.argsort(short_order, axis=-1, stable=True)[:, :, :half_cap] + half_pref
    chosen = jnp.concatenate([long_chosen, short_chosen], axis=-1)
    candidates = (jnp.arange(N_GRP)[None, :, None] * PREF + chosen).reshape(N_GRP, N_GRP * CAP)
    favoured = jax.random.randint(favour_key, (N_GRP, 1), 0, N_GRP)
    owner_of = jnp.repeat(jnp.arange(N_GRP), CAP)[None, :]
    scores = jax.random.randint(score_key, (N_GRP, N_GRP * CAP), 0, 1 << 16) * (N_GRP * CAP)
    scores = scores + jnp.arange(N_GRP * CAP)[None, :] + jnp.where(owner_of == favoured, 1 << 28, 0)
    picked = jax.lax.top_k(scores, NEED)[1]
    return jnp.take_along_axis(candidates, picked, axis=1).astype(jnp.int32)


def draw_prefix_kv(key, part):
    key = jax.random.fold_in(key, 53)
    base_key = jax.random.fold_in(key, 0)
    values = jax.random.normal(base_key, (NPRE, LEN, KVH, SPLIT, 2, HALF), jnp.float32)
    return values.reshape(NPRE, LEN, 2 * KVH * HEAD).astype(jnp.bfloat16)


def strengthened(values, key, source, target, shards_of, factor):
    owner, partner = [(jnp.arange(values.shape[axis_at]) // (values.shape[axis_at] // shards_of)).reshape([-1 if axis == axis_at else 1 for axis in range(values.ndim)]) for axis_at in (source, target)]
    chosen = jax.random.permutation(key, shards_of)[partner]
    strong = (owner == chosen) | (owner == (partner + shards_of // 2) % shards_of)
    return jnp.where(strong, factor * values, values)


def steps_of(rng, dims, pieces, low, largest):
    gain, own = 1.0, jax.random.fold_in(rng, 6)
    for dim, blocks in pieces:
        steps = jnp.exp(jax.random.uniform(jax.random.fold_in(own, dim), (blocks,), jnp.float32, low / len(pieces), largest / len(pieces)))
        gain = gain * jnp.repeat(steps, dims[dim] // blocks).reshape([-1 if axis == dim else 1 for axis in range(len(dims))])
    return gain


def length_profile(amount, total, bound, slope):
    portions = [(1 << 20) // math.isqrt(standing ** slope) + 1 for standing in range(2, amount + 1)]
    spare, counts = total - bound - (amount - 1), [1] * (amount - 1)
    while spare > 0:
        free = [i for i in range(amount - 1) if counts[i] < bound]
        mass, left = sum([portions[i] for i in free]), spare
        for i in free:
            more = min(bound - counts[i], max(1, left * portions[i] // mass), spare)
            counts[i] = counts[i] + more
            spare = spare - more
    return np.array([bound] + counts)


def ragged_sizes(stream_key, amount, total, most, slope):
    if amount == 2:
        one = jax.random.randint(stream_key, (), max(1, total - most), min(most, total - 1) + 1)
        return jnp.stack([one, total - one])
    sizes = jnp.asarray(length_profile(amount, total, most, slope), jnp.int32)
    pairs = (amount - 1) // 2
    donor, taker = sizes[1:1 + 2 * pairs:2], sizes[2:2 + 2 * pairs:2]
    room = jnp.minimum(donor - 1, most - taker)
    passed = jax.random.randint(jax.random.fold_in(stream_key, 1), (pairs,), 0, 1 << 20) % (room + 1)
    sizes = sizes.at[1:1 + 2 * pairs:2].set(donor - passed).at[2:2 + 2 * pairs:2].set(taker + passed)
    return sizes[jax.random.permutation(jax.random.fold_in(stream_key, 2), amount)]


def centred(rng, shape, width, limit, shards=(), kind=jnp.bfloat16):
    entries = jax.random.normal(rng, shape, jnp.float32) * width
    if len(shards) > 0:
        entries = steps_of(rng, shape, shards, -0.22, 0.18) * entries
    return jnp.clip(entries, min=-limit, max=limit).astype(kind)


def gaussian_with(key, extent, deviation, reach, pieces, heavy, kind=jnp.bfloat16):
    result = deviation * jax.random.normal(key, extent, jnp.float32)
    if pieces:
        result = result * steps_of(key, extent, pieces, -0.22, 0.18)
    return jnp.clip(strengthened(result, jax.random.fold_in(key, 3), *heavy), -reach, reach).astype(kind)


def setup_inputs(seed: int = 0) -> dict:
    splits = jax.random.split(jax.random.key(seed), 10)
    return {
        "embedded": centred(splits[0], (STEPS, TOTAL_ROWS, D), 1.0, 6.0, ((1, 8), (2, 16))),
        "norm_gain": jnp.clip(1.0 + 0.15 * jax.random.normal(splits[1], (D,), jnp.float32), 0.25, 1.75),
        "w_query": centred(splits[2], (D, H * HEAD), D ** -0.5, 0.0625, ((1, 16),)),
        "w_keyval": centred(splits[3], (D, 2 * KVH * HEAD), D ** -0.5, 0.0625, ((1, 16),)),
        "w_out": gaussian_with(splits[4], (H * HEAD, D), HEAD ** -0.5, 0.75, ((0, 16),), (0, 1, 16, 2.0)),
        "prefix_kv": draw_prefix_kv(jax.random.fold_in(splits[9], 71), 0),
        "prefix_len": draw_prefix_len(jax.random.fold_in(splits[9], 71), 0),
        "needed": draw_needed(jax.random.fold_in(splits[9], 71), 0),
        "row_slot": jax.vmap(lambda own: jnp.searchsorted(jnp.cumsum(ragged_sizes(own, NEED, ROWS, MOST, 1)), jnp.arange(ROWS), side="right"))(jax.random.split(splits[8], N_GRP)).reshape((N_GRP, ROWS)).astype(jnp.int32),
    }


EPSILON = 1e-05
ROPE_THETA = 500000.0

def rotate(values, positions, first_dim):
    half_count = values.shape[-1] // 2
    pair_index = (first_dim // 2 + jnp.arange(half_count)).astype(jnp.float32)
    inverse = jnp.exp(pair_index * (-2.0 * math.log(ROPE_THETA) / HEAD))
    angle = positions.astype(jnp.float32)[:, None, None] * inverse[None, None, :]
    cosine = jnp.cos(angle)
    sine = jnp.sin(angle)
    evens = values[..., 0::2]
    odds = values[..., 1::2]
    turned = jnp.stack([evens * cosine - odds * sine, evens * sine + odds * cosine], axis=-1)
    return turned.reshape(values.shape)

def reference(embedded, norm_gain, w_query, w_keyval, w_out, prefix_kv, prefix_len, needed, row_slot):
    grouped = H // KVH
    inv_sqrt = 1.0 / math.sqrt(HEAD)
    layout = w_keyval.reshape(D, KVH, SPLIT, 2, HALF)
    w_key = layout[:, :, :, 0, :].reshape(D, KVH * HEAD)
    w_value = layout[:, :, :, 1, :].reshape(D, KVH * HEAD)
    cached = prefix_kv.reshape(NPRE, LEN, KVH, SPLIT, 2, HALF)
    key_table = cached[:, :, :, :, 0, :].reshape(NPRE, LEN, KVH, HEAD).astype(jnp.float32)
    value_table = cached[:, :, :, :, 1, :].reshape(NPRE, LEN, KVH, HEAD).astype(jnp.float32)
    prefix_ids = jnp.take_along_axis(needed, row_slot, axis=1).reshape(-1).astype(jnp.int32)
    base_positions = prefix_len[prefix_ids]
    own_keys = []
    own_values = []
    outputs = []
    for step_index in range(STEPS):
        stream_rows = embedded[step_index].astype(jnp.float32)
        inv_rms = lax.rsqrt(lax.optimization_barrier(jnp.mean(stream_rows * stream_rows, axis=1, keepdims=True)) + EPSILON)
        normed = (stream_rows * inv_rms * norm_gain[None, :]).astype(jnp.bfloat16)
        positions = base_positions + step_index
        queries = jnp.dot(normed, w_query, preferred_element_type=jnp.float32).reshape(TOTAL_ROWS, H, HEAD)
        queries = rotate(queries, positions, 0).astype(jnp.bfloat16)
        new_keys = jnp.dot(normed, w_key, preferred_element_type=jnp.float32).reshape(TOTAL_ROWS, KVH, HEAD)
        new_keys = rotate(new_keys, positions, 0).astype(jnp.bfloat16)
        new_values = jnp.dot(normed, w_value, preferred_element_type=jnp.float32).reshape(TOTAL_ROWS, KVH, HEAD).astype(jnp.bfloat16)
        own_keys.append(new_keys)
        own_values.append(new_values)
        key_stack = jnp.stack(own_keys, axis=1)
        value_stack = jnp.stack(own_values, axis=1)

        def attend_row(row_inputs):
            query_row, prefix_id, key_row, value_row = row_inputs
            keys_here = lax.dynamic_index_in_dim(key_table, prefix_id, 0, keepdims=False)
            values_here = lax.dynamic_index_in_dim(value_table, prefix_id, 0, keepdims=False)
            length_here = lax.dynamic_index_in_dim(prefix_len, prefix_id, 0, keepdims=False)
            heads = query_row.astype(jnp.float32).reshape(KVH, grouped, HEAD)
            scores = jnp.einsum('kgd,lkd->kgl', heads, keys_here) * inv_sqrt
            in_range = jnp.arange(LEN)[None, None, :] < length_here
            scores = jnp.where(in_range, scores, -jnp.inf)
            own_scores = jnp.einsum('kgd,skd->kgs', heads, key_row.astype(jnp.float32)) * inv_sqrt
            row_max = jnp.maximum(lax.optimization_barrier(jnp.max(scores, axis=-1)), lax.optimization_barrier(jnp.max(own_scores, axis=-1)))[..., None]
            weights = jnp.exp(scores - row_max)
            own_weights = jnp.exp(own_scores - row_max)
            denominator = lax.optimization_barrier(jnp.sum(weights, axis=-1)) + lax.optimization_barrier(jnp.sum(own_weights, axis=-1))
            rounded = lax.optimization_barrier(weights.astype(jnp.bfloat16)).astype(jnp.float32)
            own_rounded = lax.optimization_barrier(own_weights.astype(jnp.bfloat16)).astype(jnp.float32)
            summed = jnp.einsum('kgl,lkd->kgd', rounded, values_here)
            summed = summed + jnp.einsum('kgs,skd->kgd', own_rounded, value_row.astype(jnp.float32))
            return (summed / denominator[..., None]).astype(jnp.bfloat16).reshape(H * HEAD)
        attended = lax.map(attend_row, (queries, prefix_ids, key_stack, value_stack))
        projected = jnp.dot(attended, w_out, preferred_element_type=jnp.float32)
        outputs.append((stream_rows + projected).astype(jnp.bfloat16))
    return jnp.stack(outputs)
```

```python
import functools
import math

import jax
import jax.numpy as jnp
from jax import lax
from jax.experimental import pallas as pl
from jax.experimental.pallas import tpu as pltpu
from jax.sharding import PartitionSpec as P

HEAD = 128
HALF = 64
RING = 4
EPSILON = 1e-05
ROPE_THETA = 500000.0
SUB = 32
MIB = 1 << 20
MESH = pl.DeviceIdType.MESH
ORDER = (0, 3, 1, 2)


def place():
    t = lax.axis_index("tp")
    return t, lax.div(t, RING), lax.rem(t, RING)


def index_of(x, z):
    return lax.rem(x, RING) * RING + lax.rem(z, RING)


def greet(x, z):
    barrier = pltpu.get_barrier_semaphore()
    for a, b in ((1, 0), (3, 0), (0, 1), (0, 3)):
        pl.semaphore_signal(
            barrier, inc=1, device_id={"tp": index_of(x + a, z + b)}, device_id_type=MESH
        )
    pl.semaphore_wait(barrier, 4)


def project_kernel(
    emb, wq, wkv, gain, table, slots, q_out, kv_out,
    blocks, w, acc, squares, cosine, sine, kv_other,
    load_sem, w_sem, send_sem, recv_sem, kv_sem,
):
    rows, width = emb.shape[1], emb.shape[2]
    half = rows // 2
    q_cols = wq.shape[1]
    t, x, z = place()

    def slot_of(s, along, across):
        return index_of(x + across, z + along) if s == 0 else index_of(x + along, z + across)

    def neighbour(s, phase, d):
        on_z = (s == 0) == (phase == 0)
        return {"tp": index_of(x, z + d) if on_z else index_of(x + d, z)}

    def move(s, phase, o, kind, slot, d):
        ref = blocks.at[s, slot]
        if kind == 2:
            ref = blocks.at[s, slot, pl.ds(0, half)]
        if kind == 3:
            ref = blocks.at[s, slot, pl.ds(half, half)]
        i = o if phase else RING
        return pltpu.make_async_remote_copy(
            src_ref=ref,
            dst_ref=ref,
            send_sem=send_sem.at[s, i, kind],
            recv_sem=recv_sem.at[s, i, kind],
            device_id=neighbour(s, phase, d),
            device_id_type=MESH,
        )

    def at(s, phase, o, far):
        return slot_of(s, far, 0) if phase == 0 else slot_of(s, ORDER[o], far)

    started = []

    def start(*a):
        copy = move(*a)
        copy.start()
        started.append(copy)

    def send(s, phase, o):
        slot = at(s, phase, o, 0)
        start(s, phase, o, 0, slot, 1)
        start(s, phase, o, 1, slot, RING - 1)

    def pass_on(s, phase, o):
        back, ahead = at(s, phase, o, 3), at(s, phase, o, 1)
        move(s, phase, o, 0, back, 1).wait_recv()
        start(s, phase, o, 2, back, 1)
        move(s, phase, o, 1, ahead, 1).wait_recv()
        start(s, phase, o, 3, ahead, RING - 1)

    def opposite(s, phase, o):
        slot = at(s, phase, o, 2)
        move(s, phase, o, 2, slot, 1).wait_recv()
        move(s, phase, o, 3, slot, 1).wait_recv()

    def multiply(*todo):
        def one(i, _):
            which = lax.div(i, 2)
            s, slot = jnp.int32(todo[0][0]), todo[0][1]
            for j in range(1, len(todo)):
                s = jnp.where(which == j, todo[j][0], s)
                slot = jnp.where(which == j, todo[j][1], slot)
            r = pl.ds(pl.multiple_of(lax.rem(i, 2) * half, half), half)
            value = blocks[s, slot, r, :].astype(jnp.float32)
            square = value * value
            total = square[:, :128]
            for c in range(1, width // 128):
                total = total + square[:, c * 128 : (c + 1) * 128]
            squares[s, r, :] += total
            scaled = (value * gain[pl.ds(slot, 1), :]).astype(jnp.bfloat16)
            depth = pl.ds(pl.multiple_of(slot * width, width), width)
            acc[s, r, :] += jnp.dot(scaled, w[depth, :], preferred_element_type=jnp.float32)
            return 0

        lax.fori_loop(0, 2 * len(todo), one, 0)

    greet(x, z)
    loads = [pltpu.make_async_copy(emb.at[s], blocks.at[s, t], load_sem.at[s]) for s in (0, 1)]
    for copy in loads:
        copy.start()
    weights = [
        pltpu.make_async_copy(wq, w.at[:, pl.ds(0, q_cols)], w_sem.at[0]),
        pltpu.make_async_copy(wkv, w.at[:, pl.ds(q_cols, 2 * HALF)], w_sem.at[1]),
    ]
    for copy in loads:
        copy.wait()
    for s in (0, 1):
        send(s, 0, 0)
    for copy in weights:
        copy.start()
    for s in (0, 1):
        send(s, 1, 0)
    acc[...] = jnp.zeros_like(acc)
    squares[...] = jnp.zeros_like(squares)

    def spread(i, _):
        s, r = lax.div(i, 4), pl.ds(pl.multiple_of(lax.rem(i, 4) * 128, 128), 128)
        slot_here = jnp.broadcast_to(slots[r, :], (128, HEAD))
        for k, ref in ((0, cosine), (1, sine)):
            out = jnp.zeros((128, HEAD), jnp.float32)
            for n in range(table.shape[2]):
                out = jnp.where(slot_here == n, table[k, s, n : n + 1, :], out)
            ref[s, r, :] = out
        return 0

    lax.fori_loop(0, 8, spread, 0)
    for copy in weights:
        copy.wait()
    both = (0, 1)
    multiply((0, t), (1, t))
    for s in both:
        pass_on(s, 0, 0)
    for s in both:
        send(s, 1, 1)
    for s in both:
        send(s, 1, 2)
    multiply(*[(s, at(s, 0, 0, d)) for d in (3, 1) for s in both])
    for s in both:
        pass_on(s, 1, 0)
    multiply(*[(s, at(s, 1, 0, d)) for d in (3, 1) for s in both])
    for s in both:
        opposite(s, 0, 0)
        send(s, 1, 3)
    multiply(*[(s, at(s, 0, 0, 2)) for s in both])
    for o in (1, 2, 3):
        for s in both:
            pass_on(s, 1, o)
        multiply(*[(s, at(s, 1, o, d)) for d in (3, 1) for s in both])
        for s in both:
            opposite(s, 1, o - 1)
        multiply(*[(s, at(s, 1, o - 1, 2)) for s in both])
    for s in both:
        opposite(s, 1, 3)
    multiply(*[(s, at(s, 1, 3, 2)) for s in both])

    upper = lax.rem(t, 2)
    lane = lax.broadcasted_iota(jnp.int32, (128, HEAD), 1)
    low = lane < HALF
    even = lax.rem(lane, 2) == 0

    def turn(v, c, n):
        other = jnp.where(even, pltpu.roll(v, HEAD - 1, 1), pltpu.roll(v, 1, 1))
        return v * c + other * n

    def scale_of(s, r):
        mean = jnp.sum(squares[s, r, :], axis=1, keepdims=True) / (RING * RING * width)
        return lax.rsqrt(mean + EPSILON)

    def own_kv(i, _):
        s, r = lax.div(i, 4), pl.ds(pl.multiple_of(lax.rem(i, 4) * 128, 128), 128)
        v = acc[s, r, pl.ds(q_cols, HEAD)] * scale_of(s, r)
        c, n = cosine[s, r, :], sine[s, r, :]
        c = jnp.where(upper == 0, c, pltpu.roll(c, HALF, 1))
        n = jnp.where(upper == 0, n, pltpu.roll(n, HALF, 1))
        v = jnp.where(low, turn(v, c, n), v)
        kv_out[s, r, pl.ds(0, HEAD)] = v.astype(jnp.bfloat16)
        return 0

    lax.fori_loop(0, 8, own_kv, 0)
    swap = pltpu.make_async_remote_copy(
        src_ref=kv_out.at[:, :, pl.ds(0, HEAD)],
        dst_ref=kv_other,
        send_sem=kv_sem.at[0],
        recv_sem=kv_sem.at[1],
        device_id={"tp": t + 1 - 2 * upper},
        device_id_type=MESH,
    )
    swap.start()

    def queries(i, _):
        s, r = lax.div(i, 4), pl.ds(pl.multiple_of(lax.rem(i, 4) * 128, 128), 128)
        scale = scale_of(s, r)
        c, n = cosine[s, r, :], sine[s, r, :]
        for h in range(q_cols // HEAD):
            v = turn(acc[s, r, pl.ds(h * HEAD, HEAD)] * scale, c, n)
            rolled = pltpu.roll(v, HALF, 1)
            first = jnp.where(low, jnp.where(upper == 0, v, rolled), 0.0)
            second = jnp.where(low, jnp.where(upper == 0, rolled, v), 0.0)
            q_out[s, r, pl.ds(2 * h * HEAD, HEAD)] = first.astype(jnp.bfloat16)
            q_out[s, r, pl.ds((2 * h + 1) * HEAD, HEAD)] = second.astype(jnp.bfloat16)
        return 0

    lax.fori_loop(0, 8, queries, 0)
    swap.wait()
    kv_out[:, :, pl.ds(HEAD, HEAD)] = kv_other[...]
    for copy in started:
        copy.wait_send()


def project(emb, wq, wkv, gain, table, slots):
    steps, rows, width = emb.shape
    q_cols = wq.shape[1]
    heads = q_cols // HEAD
    vmem = pl.BlockSpec(memory_space=pltpu.VMEM)
    hbm = pl.BlockSpec(memory_space=pl.ANY)
    tp = RING * RING
    return pl.pallas_call(
        project_kernel,
        out_shape=(
            jax.ShapeDtypeStruct((steps, rows, heads * 2 * HEAD), jnp.bfloat16),
            jax.ShapeDtypeStruct((steps, rows, 2 * HEAD), jnp.bfloat16),
        ),
        in_specs=[hbm, hbm, hbm, vmem, vmem, vmem],
        out_specs=(vmem, vmem),
        scratch_shapes=[
            pltpu.VMEM((steps, tp, rows, width), jnp.bfloat16),
            pltpu.VMEM((tp * width, q_cols + HEAD), jnp.bfloat16),
            pltpu.VMEM((steps, rows, q_cols + HEAD), jnp.float32),
            pltpu.VMEM((steps, rows, HEAD), jnp.float32),
            pltpu.VMEM((steps, rows, HEAD), jnp.float32),
            pltpu.VMEM((steps, rows, HEAD), jnp.float32),
            pltpu.VMEM((steps, rows, HEAD), jnp.bfloat16),
            pltpu.SemaphoreType.DMA((2,)),
            pltpu.SemaphoreType.DMA((2,)),
            pltpu.SemaphoreType.DMA((2, RING + 1, 4)),
            pltpu.SemaphoreType.DMA((2, RING + 1, 4)),
            pltpu.SemaphoreType.DMA((2,)),
        ],
        compiler_params=pltpu.CompilerParams(
            collective_id=0, has_side_effects=True, vmem_limit_bytes=48 * MIB
        ),
        cost_estimate=pl.CostEstimate(
            flops=2 * steps * rows * tp * width * (q_cols + HEAD),
            bytes_accessed=300 * MIB,
            transcendentals=0,
        ),
        name="project",
    )(emb, wq, wkv, gain, table, slots)


def attend_kernel(first_b, second_b, length, begin, end, upper_ref, q, own, kv0, kv1, out):
    slot = pl.program_id(0)
    steps = q.shape[0]
    heads = q.shape[2] // (2 * HEAD)
    many = steps * heads * SUB
    n_keys = length[slot]
    lo, hi = begin[slot], end[slot]
    upper = upper_ref[0]
    factor = math.log2(math.e) / math.sqrt(HEAD)
    nt = (((1,), (1,)), ((), ()))

    def tile(i, long):
        r0 = pl.multiple_of(i * SUB, SUB)
        r = pl.ds(r0, SUB)
        query = jnp.concatenate(
            [q[s, r, pl.ds(h * 2 * HEAD, 2 * HEAD)] for s in range(steps) for h in range(heads)],
            axis=0,
        )
        mine = jnp.concatenate([own[s, r, :] for s in range(steps)], axis=0)
        pieces = [kv0[0], kv1[0]] if long else [kv0[0]]
        row = lax.broadcasted_iota(jnp.int32, (many, steps * SUB), 0)
        col = lax.broadcasted_iota(jnp.int32, (many, steps * SUB), 1)
        allowed = (lax.rem(row, SUB) == lax.rem(col, SUB)) & (
            lax.div(col, SUB) <= lax.div(row, heads * SUB)
        )
        scores = [
            jnp.where(
                allowed,
                lax.dot_general(query, mine, nt, preferred_element_type=jnp.float32),
                -jnp.inf,
            )
        ]
        for n, piece in enumerate(pieces):
            raw = lax.dot_general(query, piece, nt, preferred_element_type=jnp.float32)
            key = lax.broadcasted_iota(jnp.int32, raw.shape, 1) + n * piece.shape[0]
            scores.append(jnp.where(key < n_keys, raw, -jnp.inf))
        top = functools.reduce(
            jnp.maximum, [jnp.max(part, axis=1, keepdims=True) for part in scores]
        )
        total = jnp.zeros((many, 1), jnp.float32)
        summed = jnp.zeros((many, 2 * HEAD), jnp.float32)
        for part, piece in zip(scores, [mine] + pieces):
            weight = jnp.exp2((part - top) * factor)
            total = total + jnp.sum(weight, axis=1, keepdims=True)
            summed = summed + jnp.dot(
                weight.astype(jnp.bfloat16), piece, preferred_element_type=jnp.float32
            )
        summed = summed / total
        here, there = summed[:, :HEAD], summed[:, HEAD:]
        low = lax.broadcasted_iota(jnp.int32, here.shape, 1) < HALF
        first = jnp.where(upper == 0, here, there)
        second = jnp.where(upper == 0, there, here)
        result = jnp.where(low, pltpu.roll(first, HALF, 1), second)
        at_row = lax.broadcasted_iota(jnp.int32, (SUB, HEAD), 0) + r0
        inside = (at_row >= lo) & (at_row < hi)
        for s in range(steps):
            for h in range(heads):
                j = (s * heads + h) * SUB
                c = pl.ds(h * HEAD, HEAD)
                before = out[s, r, c].astype(jnp.float32)
                out[s, r, c] = jnp.where(inside, result[j : j + SUB], before).astype(jnp.bfloat16)
        return 0

    from_tile = lax.div(lo, SUB)
    to_tile = lax.div(hi + SUB - 1, SUB)

    @pl.when(n_keys > kv0.shape[1])
    def _():
        lax.fori_loop(from_tile, to_tile, lambda i, c: tile(i, True), 0)

    @pl.when(n_keys <= kv0.shape[1])
    def _():
        lax.fori_loop(from_tile, to_tile, lambda i, c: tile(i, False), 0)


def attend(q, own, cache, first_b, second_b, length, begin, end, upper):
    steps, rows, wide = q.shape
    whole = lambda shape: pl.BlockSpec(shape, lambda i, *_: (0,) * len(shape))
    block = (1,) + cache.shape[1:]
    return pl.pallas_call(
        attend_kernel,
        out_shape=jax.ShapeDtypeStruct((steps, rows, wide // 2), jnp.bfloat16),
        grid_spec=pltpu.PrefetchScalarGridSpec(
            num_scalar_prefetch=6,
            grid=(length.shape[0],),
            in_specs=[
                whole(q.shape),
                whole(own.shape),
                pl.BlockSpec(block, lambda i, a, b, *_: (a[i], 0, 0)),
                pl.BlockSpec(block, lambda i, a, b, *_: (b[i], 0, 0)),
            ],
            out_specs=whole((steps, rows, wide // 2)),
        ),
        compiler_params=pltpu.CompilerParams(vmem_limit_bytes=32 * MIB),
        cost_estimate=pl.CostEstimate(
            flops=8 * 10**9, bytes_accessed=60 * MIB, transcendentals=5 * 10**6
        ),
        name="attend",
    )(first_b, second_b, length, begin, end, upper, q, own, cache, cache)


def output_kernel(
    a, wo, emb, out, gathered, w, away, back,
    load_sem, w_sem, ag_send, ag_recv, rs_send, rs_recv, chunks,
):
    rows, depth = a.shape[0] // chunks, a.shape[1]
    cols = out.shape[1]
    t, x, z = place()

    def at(r):
        return pl.ds(pl.multiple_of(r * rows, rows), rows)

    def line(d):
        return {"tp": index_of(x + d, z)}

    def column(d):
        return {"tp": index_of(x, z + d)}

    def share(r, k, d):
        return pltpu.make_async_remote_copy(
            src_ref=gathered.at[0, at(r)],
            dst_ref=gathered.at[k, at(r)],
            send_sem=ag_send.at[r, k - 1],
            recv_sem=ag_recv.at[r, k - 1],
            device_id=line(d),
            device_id_type=MESH,
        )

    def forward(r, d):
        return pltpu.make_async_remote_copy(
            src_ref=gathered.at[d, at(r)],
            dst_ref=gathered.at[2, at(r)],
            send_sem=ag_send.at[r, 1],
            recv_sem=ag_recv.at[r, 1],
            device_id=line(d),
            device_id_type=MESH,
        )

    def give(r, n, d):
        return pltpu.make_async_remote_copy(
            src_ref=away.at[n, at(r)],
            dst_ref=back.at[n, at(r)],
            send_sem=rs_send.at[r, n],
            recv_sem=rs_recv.at[r, n],
            device_id=column(d),
            device_id_type=MESH,
        )

    def product(r, d):
        c = pl.ds(pl.multiple_of(lax.rem(z + d, RING) * cols, cols), cols)
        total = None
        for k in range(RING):
            part = jnp.dot(
                gathered[k, at(r), :],
                w[k, :, :, c].reshape(depth, cols),
                preferred_element_type=jnp.float32,
            )
            total = part if total is None else total + part
        return total

    def offer(r):
        share(r, 1, 1).start()
        share(r, 3, RING - 1).start()

    def arrive(r, d):
        share(r, 1, 1).wait_recv()
        share(r, 3, RING - 1).wait_recv()
        forward(r, d).start()

    greet(x, z)
    load = pltpu.make_async_copy(a, gathered.at[0], load_sem)
    load.start()
    load.wait()
    weights = [pltpu.make_async_copy(wo.at[:, k], w.at[k], w_sem.at[k]) for k in range(RING)]
    offer(0)
    offer(1)
    for copy in weights:
        copy.start()
    offer(2)
    arrive(0, 1)
    for copy in weights:
        copy.wait()

    def step(j, _):
        for parity in (0, 1):
            r = 2 * j + parity
            d = (1, RING - 1)[parity]
            e = RING - d

            @pl.when(r + 1 < chunks)
            def _():
                @pl.when(r + 3 < chunks)
                def _():
                    offer(r + 3)

                arrive(r + 1, e)

            @pl.when(r < chunks)
            def _():
                forward(r, d).wait_recv()
                away[0, at(r), :] = product(r, 2).astype(jnp.bfloat16)
                give(r, 0, d).start()
                away[2, at(r), :] = product(r, e).astype(jnp.bfloat16)
                give(r, 2, e).start()

            @pl.when((r >= 1) & (r <= chunks))
            def _():
                before = r - 1
                give(before, 0, e).wait_recv()
                total = product(before, e) + back[0, at(before), :].astype(jnp.float32)
                away[1, at(before), :] = total.astype(jnp.bfloat16)
                give(before, 1, e).start()

            @pl.when((r >= 2) & (r <= chunks + 1))
            def _():
                before = r - 2
                total = product(before, 0) + emb[at(before), :].astype(jnp.float32)
                give(before, 2, d).wait_recv()
                total = total + back[2, at(before), :].astype(jnp.float32)
                give(before, 1, d).wait_recv()
                total = total + back[1, at(before), :].astype(jnp.float32)
                out[at(before), :] = total.astype(jnp.bfloat16)

        return 0

    lax.fori_loop(0, chunks // 2 + 1, step, 0)

    def finish(r, _):
        share(r, 1, 1).wait_send()
        share(r, 3, RING - 1).wait_send()
        forward(r, 1).wait_send()
        for n in range(3):
            give(r, n, 1).wait_send()
        return 0

    lax.fori_loop(0, chunks, finish, 0)


def output(a, wo, emb, chunks):
    rows, depth = a.shape
    cols = emb.shape[1]
    vmem = pl.BlockSpec(memory_space=pltpu.VMEM)
    hbm = pl.BlockSpec(memory_space=pl.ANY)
    dma = pltpu.SemaphoreType.DMA
    return pl.pallas_call(
        functools.partial(output_kernel, chunks=chunks),
        out_shape=jax.ShapeDtypeStruct((rows, cols), jnp.bfloat16),
        in_specs=[hbm, hbm, vmem],
        out_specs=vmem,
        scratch_shapes=[
            pltpu.VMEM((RING, rows, depth), jnp.bfloat16),
            pltpu.VMEM((RING,) + wo.shape[:1] + wo.shape[2:], jnp.bfloat16),
            pltpu.VMEM((3, rows, cols), jnp.bfloat16),
            pltpu.VMEM((3, rows, cols), jnp.bfloat16),
            dma,
            dma((RING,)),
            dma((chunks, 3)),
            dma((chunks, 3)),
            dma((chunks, 3)),
            dma((chunks, 3)),
        ],
        compiler_params=pltpu.CompilerParams(
            collective_id=1, has_side_effects=True, vmem_limit_bytes=48 * MIB
        ),
        cost_estimate=pl.CostEstimate(
            flops=2 * rows * depth * RING * RING * cols, bytes_accessed=150 * MIB, transcendentals=0
        ),
        name="output",
    )(a, wo, emb)


def body(embedded, norm_gain, w_query, w_keyval, w_out, prefix_kv, prefix_len, needed, row_slot):
    group = lax.axis_index("grp")
    groups = lax.axis_size("grp")
    t, x, z = place()
    steps, rows, width = embedded.shape
    owned, longest, kv_width = prefix_kv.shape
    short = longest // 2
    n_long = owned // 2

    mine = jnp.concatenate(
        [
            prefix_kv[:n_long].reshape(2 * n_long, short, kv_width),
            prefix_kv[n_long:, :short],
        ]
    )
    theirs = lax.ppermute(mine, "tp", [(i, i ^ 1) for i in range(RING * RING)])
    per_owner = mine.shape[0]
    cache = lax.all_gather(jnp.concatenate([mine, theirs], axis=2), "grp", axis=0, tiled=True)

    piece_rows = w_out.shape[0] // groups
    quarter = w_out.shape[1] // RING
    pieces = []
    for k in range(RING):
        piece = lax.dynamic_slice(
            w_out, (group * piece_rows, lax.rem(x + k, RING) * quarter), (piece_rows, quarter)
        )
        if k:
            route = [
                (i, (i // RING + k) % RING * RING + i % RING) for i in range(RING * RING)
            ]
            piece = lax.ppermute(piece, "tp", route)
        pieces.append(piece)
    wo = lax.all_gather(jnp.stack(pieces), "grp", axis=0)

    ids = lax.dynamic_index_in_dim(needed, group, 0, keepdims=False)
    slots = ids.shape[0]
    match = ids[:, None] == jnp.arange(prefix_len.shape[0])[None, :]
    slot_len = jnp.sum(jnp.where(match, prefix_len[None, :], 0), axis=1)
    owner = ids // owned
    local = ids - owner * owned
    is_long = local < n_long
    first_b = owner * per_owner + jnp.where(is_long, 2 * local, local + n_long)
    second_b = first_b + is_long.astype(jnp.int32)
    slot_of_row = row_slot[0]
    names = jnp.arange(slots)[:, None]
    begin = jnp.sum((slot_of_row[None, :] < names).astype(jnp.int32), axis=1)
    end = jnp.sum((slot_of_row[None, :] <= names).astype(jnp.int32), axis=1)

    pair = (jnp.arange(HEAD) // 2).astype(jnp.float32)
    inverse = jnp.exp(pair * (-2.0 * math.log(ROPE_THETA) / HEAD))
    position = (slot_len[None, :] + jnp.arange(steps)[:, None]).astype(jnp.float32)
    angle = position[:, :, None] * inverse[None, None, :]
    sign = jnp.where(jnp.arange(HEAD) % 2 == 0, -1.0, 1.0)
    table = jnp.stack([jnp.cos(angle), jnp.sin(angle) * sign])

    q, own = project(
        embedded,
        w_query,
        w_keyval,
        norm_gain.reshape(RING * RING, width),
        table,
        slot_of_row[:, None],
    )
    upper = lax.rem(t, 2).astype(jnp.int32)[None]
    attended = attend(q, own, cache, first_b, second_b, slot_len, begin, end, upper)
    mixed = output(
        attended.reshape(steps * rows, width), wo, embedded.reshape(steps * rows, width), 8
    )
    return mixed.reshape(steps, rows, width)


def solution(mesh):
    in_specs = (
        P(None, "grp", "tp"),
        P(),
        P(None, "tp"),
        P(None, "tp"),
        P("tp", None),
        P("grp", None, "tp"),
        P(),
        P(),
        P("grp", None),
    )
    out_specs = P(None, "grp", "tp")
    return jax.shard_map(body, mesh=mesh, in_specs=in_specs, out_specs=out_specs, check_vma=False)
```

```python
import functools
import math

import jax
import jax.numpy as jnp
from jax import lax
from jax.experimental import pallas as pl
from jax.experimental.pallas import tpu as pltpu
from jax.sharding import PartitionSpec as P

HEAD = 128
HALF = 64
RING = 4
EPSILON = 1e-05
ROPE_THETA = 500000.0
SUB = 32
MIB = 1 << 20
MESH = pl.DeviceIdType.MESH
ORDER = (0, 3, 1, 2)


def place():
    t = lax.axis_index("tp")
    return t, lax.div(t, RING), lax.rem(t, RING)


def index_of(x, z):
    return lax.rem(x, RING) * RING + lax.rem(z, RING)


def greet(partners):
    barrier = pltpu.get_barrier_semaphore()
    for device in partners:
        pl.semaphore_signal(barrier, inc=1, device_id=device, device_id_type=MESH)
    pl.semaphore_wait(barrier, len(partners))


def around(x, z):
    return [{"tp": index_of(x + a, z + b)} for a, b in ((1, 0), (3, 0), (0, 1), (0, 3))]


def project_kernel(
    emb, wq, wkv, gain, row_slot, needed, lengths, prefix, prefix_halves, wo_here,
    q_out, kv_out, cache, wo, begin,
    blocks, w_q, w_kv, acc, squares, cosine, sine, kv_other, mine, table,
    load_sem, w_sem, send_sem, recv_sem, kv_sem, side_send, side_recv,
):
    rows, width = emb.shape[1], emb.shape[2]
    half = rows // 2
    q_cols = wq.shape[1]
    t, x, z = place()

    def slot_of(s, along, across):
        return index_of(x + across, z + along) if s == 0 else index_of(x + along, z + across)

    def neighbour(s, phase, d):
        on_z = (s == 0) == (phase == 0)
        return {"tp": index_of(x, z + d) if on_z else index_of(x + d, z)}

    def move(s, phase, o, kind, slot, d):
        ref = blocks.at[s, slot]
        if kind == 2:
            ref = blocks.at[s, slot, pl.ds(0, half)]
        if kind == 3:
            ref = blocks.at[s, slot, pl.ds(half, half)]
        i = o if phase else RING
        return pltpu.make_async_remote_copy(
            src_ref=ref,
            dst_ref=ref,
            send_sem=send_sem.at[s, i, kind],
            recv_sem=recv_sem.at[s, i, kind],
            device_id=neighbour(s, phase, d),
            device_id_type=MESH,
        )

    def at(s, phase, o, far):
        return slot_of(s, far, 0) if phase == 0 else slot_of(s, ORDER[o], far)

    started = []

    def start(*a):
        copy = move(*a)
        copy.start()
        started.append(copy)

    def send(s, phase, o):
        slot = at(s, phase, o, 0)
        start(s, phase, o, 0, slot, 1)
        start(s, phase, o, 1, slot, RING - 1)

    def pass_on(s, phase, o):
        back, ahead = at(s, phase, o, 3), at(s, phase, o, 1)
        move(s, phase, o, 0, back, 1).wait_recv()
        start(s, phase, o, 2, back, 1)
        move(s, phase, o, 1, ahead, 1).wait_recv()
        start(s, phase, o, 3, ahead, RING - 1)

    def opposite(s, phase, o):
        slot = at(s, phase, o, 2)
        move(s, phase, o, 2, slot, 1).wait_recv()
        move(s, phase, o, 3, slot, 1).wait_recv()

    def multiply(*todo):
        def one(i, _):
            which = lax.div(i, 2)
            s, slot = jnp.int32(todo[0][0]), todo[0][1]
            for j in range(1, len(todo)):
                s = jnp.where(which == j, todo[j][0], s)
                slot = jnp.where(which == j, todo[j][1], slot)
            r = pl.ds(pl.multiple_of(lax.rem(i, 2) * half, half), half)
            value = blocks[s, slot, r, :].astype(jnp.float32)
            square = value * value
            total = square[:, :128]
            for c in range(1, width // 128):
                total = total + square[:, c * 128 : (c + 1) * 128]
            squares[s, r, :] += total
            depth = pl.ds(pl.multiple_of(slot * width, width), width)
            scaled = (value * gain[:, depth]).astype(jnp.bfloat16)
            for ref, c in ((w_q, pl.ds(0, q_cols)), (w_kv, pl.ds(q_cols, HEAD))):
                acc[s, r, c] += jnp.dot(
                    scaled, ref[depth, :], preferred_element_type=jnp.float32
                )
            return 0

        lax.fori_loop(0, 2 * len(todo), one, 0)

    g = lax.axis_index("grp")
    y, core = lax.div(g, 2), lax.rem(g, 2)
    upper = lax.rem(t, 2)
    n_short = prefix_halves.shape[0] // 2
    n_long = 2 * n_short
    piece = wo.shape[2]
    quarter = wo.shape[3]
    cut = piece // 2
    other_half = {"tp": t + 1 - 2 * upper}
    sibling = {"grp": g + 1 - 2 * core}

    def group(a, flip=False):
        return lax.rem(y + a, RING) * 2 + (1 - core if flip else core)

    def up(d):
        return {"grp": group(d)}

    def side(n, src, dst, device):
        return pltpu.make_async_remote_copy(
            src_ref=src,
            dst_ref=dst,
            send_sem=side_send.at[n],
            recv_sem=side_recv.at[n],
            device_id=device,
            device_id_type=MESH,
        )

    def go(copy):
        copy.start()
        started.append(copy)

    def pair():
        return side(0, mine, cache.at[1, g], other_half)

    def cache_ring(h, d, group_id):
        ref = cache.at[h, group_id]
        return side(1 + 2 * h + (0 if d == 1 else 1), ref if h else mine, ref, up(d))

    def cache_forward(h, group_id):
        ref = cache.at[h, group_id]
        return side(5 + h, ref, ref, up(1 if h == 0 else RING - 1))

    def cache_sibling(h, a, flip=False):
        ref = cache.at[h, group(a, flip)]
        return side(7 + 4 * h + a, ref if h or a else mine, ref, sibling)

    def wo_line(k):
        c = pl.ds(pl.multiple_of(lax.rem(x + k, RING) * quarter, quarter), quarter)
        return side(
            14 + k, wo_here.at[g, :, c], wo.at[g, k - 1], {"tp": index_of(x + k, z)}
        )

    def wo_ring(d, group_id):
        ref = wo.at[group_id]
        return side(18 if d == 1 else 19, ref, ref, up(d))

    def wo_forward(d, group_id):
        ref = wo.at[group_id, :, pl.ds(0 if d == 1 else cut, cut)]
        return side(20 if d == 1 else 21, ref, ref, up(d))

    def wo_sibling(a, flip=False):
        ref = wo.at[group(a, flip)]
        return side(22 + a, ref, ref, sibling)

    ahead, back = 1, RING - 1

    def side_begin():
        go(pair())
        for d in (ahead, back):
            go(cache_ring(0, d, g))
        for k in (1, 2, 3):
            go(wo_line(k))

    def side_line():
        for k in (1, 2, 3):
            wo_line(k).wait_recv()
        for d in (ahead, back):
            go(wo_ring(d, g))
        go(wo_sibling(0))

    def side_pair():
        pair().wait_recv()
        for d in (ahead, back):
            go(cache_ring(1, d, g))
        for h in (0, 1):
            go(cache_sibling(h, 0))

    def side_cache(h):
        cache_ring(h, ahead, group(back)).wait_recv()
        if h == 0:
            go(cache_forward(h, group(back)))
        cache_ring(h, back, group(ahead)).wait_recv()
        if h == 1:
            go(cache_forward(h, group(ahead)))
        go(cache_sibling(h, back))
        go(cache_sibling(h, ahead))

    def side_wo():
        wo_ring(ahead, group(back)).wait_recv()
        go(wo_forward(ahead, group(back)))
        wo_ring(back, group(ahead)).wait_recv()
        go(wo_forward(back, group(ahead)))
        go(wo_sibling(back))
        go(wo_sibling(ahead))

    def side_cache_far(h):
        cache_forward(h, group(2)).wait_recv()
        go(cache_sibling(h, 2))

    def side_wo_far():
        wo_forward(ahead, group(2)).wait_recv()
        wo_forward(back, group(2)).wait_recv()
        go(wo_sibling(2))

    def side_end():
        for a in range(RING):
            for h in (0, 1):
                cache_sibling(h, a, True).wait_recv()
            wo_sibling(a, True).wait_recv()

    greet(
        around(x, z)
        + [{"tp": index_of(x + 2, z)}, sibling, up(ahead), up(back)]
    )
    loads = [pltpu.make_async_copy(emb.at[s], blocks.at[s, t], load_sem.at[s]) for s in (0, 1)]
    own_cache = [
        pltpu.make_async_copy(
            prefix.at[pl.ds(0, n_long)], mine.at[pl.ds(0, n_long)], load_sem.at[2]
        ),
        pltpu.make_async_copy(
            prefix_halves.at[pl.ds(n_short, n_short), 0],
            mine.at[pl.ds(n_long, n_short)],
            load_sem.at[3],
        ),
    ]
    for copy in loads + own_cache:
        copy.start()
    weights = [
        pltpu.make_async_copy(wq, w_q, w_sem.at[0]),
        pltpu.make_async_copy(wkv, w_kv, w_sem.at[1]),
    ]
    for copy in loads:
        copy.wait()
    for s in (0, 1):
        send(s, 0, 0)
    for copy in own_cache:
        copy.wait()
    side_begin()
    keep = pltpu.make_async_copy(mine, cache.at[0, g], load_sem.at[4])
    keep.start()
    for copy in weights:
        copy.start()
    for s in (0, 1):
        send(s, 1, 0)
    acc[...] = jnp.zeros_like(acc)
    squares[...] = jnp.zeros_like(squares)

    names = table.shape[1] // 2
    line = lax.broadcasted_iota(jnp.int32, (2 * names, HEAD), 0)
    lane = lax.broadcasted_iota(jnp.int32, (2 * names, HEAD), 1)
    position = jnp.zeros((2 * names, HEAD), jnp.int32)
    starts = []
    for n in range(names):
        length = lengths[needed[g, n]]
        position = jnp.where(line == n, length, position)
        position = jnp.where(line == names + n, length + 1, position)
        starts.append(jnp.sum(jnp.where(row_slot[...] < n, 1, 0)))
        begin[n] = starts[n]
    pair_index = lax.div(lane, 2).astype(jnp.float32)
    inverse = jnp.exp(pair_index * (-2.0 * math.log(ROPE_THETA) / HEAD))
    angle = position.astype(jnp.float32) * inverse
    table[0] = jnp.cos(angle)
    table[1] = jnp.sin(angle) * jnp.where(lax.rem(lane, 2) == 0, -1.0, 1.0)

    def spread(i, _):
        s, r0 = lax.div(i, 4), pl.multiple_of(lax.rem(i, 4) * 128, 128)
        row = lax.broadcasted_iota(jnp.int32, (128, HEAD), 0) + r0
        for k, ref in ((0, cosine), (1, sine)):
            out = jnp.zeros((128, HEAD), jnp.float32)
            for n in range(names):
                out = jnp.where(row >= starts[n], table[k, pl.ds(s * names + n, 1), :], out)
            ref[s, pl.ds(r0, 128), :] = out
        return 0

    lax.fori_loop(0, 8, spread, 0)
    for copy in weights:
        copy.wait()
    both = (0, 1)
    multiply((0, t), (1, t))
    for s in both:
        pass_on(s, 0, 0)
    for o in (1, 2):
        for s in both:
            send(s, 1, o)
    multiply(*[(s, at(s, 0, 0, d)) for d in (3, 1) for s in both])
    for s in both:
        pass_on(s, 1, 0)
    multiply(*[(s, at(s, 1, 0, d)) for d in (3, 1) for s in both])
    side_pair()
    for s in both:
        opposite(s, 0, 0)
        send(s, 1, 3)
    side_cache(0)
    multiply(*[(s, at(s, 0, 0, 2)) for s in both])
    side_line()
    for o in (1, 2, 3):
        for s in both:
            pass_on(s, 1, o)
        multiply(*[(s, at(s, 1, o, d)) for d in (3, 1) for s in both])
        if o == 1:
            side_cache(1)
        if o == 2:
            side_wo()
            side_cache_far(0)
        if o == 3:
            side_cache_far(1)
            side_wo_far()
        for s in both:
            opposite(s, 1, o - 1)
        multiply(*[(s, at(s, 1, o - 1, 2)) for s in both])
    for s in both:
        opposite(s, 1, 3)
    multiply(*[(s, at(s, 1, 3, 2)) for s in both])

    lane = lax.broadcasted_iota(jnp.int32, (128, HEAD), 1)
    low = lane < HALF
    even = lax.rem(lane, 2) == 0

    def turn(v, c, n):
        other = jnp.where(even, pltpu.roll(v, HEAD - 1, 1), pltpu.roll(v, 1, 1))
        return v * c + other * n

    def scale_of(s, r):
        mean = jnp.sum(squares[s, r, :], axis=1, keepdims=True) / (RING * RING * width)
        return lax.rsqrt(mean + EPSILON)

    def own_kv(i, _):
        s, r = lax.div(i, 4), pl.ds(pl.multiple_of(lax.rem(i, 4) * 128, 128), 128)
        v = acc[s, r, pl.ds(q_cols, HEAD)] * scale_of(s, r)
        c, n = cosine[s, r, :], sine[s, r, :]
        c = jnp.where(upper == 0, c, pltpu.roll(c, HALF, 1))
        n = jnp.where(upper == 0, n, pltpu.roll(n, HALF, 1))
        v = jnp.where(low, turn(v, c, n), v)
        kv_out[s, r, pl.ds(0, HEAD)] = v.astype(jnp.bfloat16)
        return 0

    lax.fori_loop(0, 8, own_kv, 0)
    swap = pltpu.make_async_remote_copy(
        src_ref=kv_out.at[:, :, pl.ds(0, HEAD)],
        dst_ref=kv_other,
        send_sem=kv_sem.at[0],
        recv_sem=kv_sem.at[1],
        device_id=other_half,
        device_id_type=MESH,
    )
    swap.start()

    def queries(i, _):
        s, r = lax.div(i, 4), pl.ds(pl.multiple_of(lax.rem(i, 4) * 128, 128), 128)
        scale = scale_of(s, r)
        c, n = cosine[s, r, :], sine[s, r, :]
        for h in range(q_cols // HEAD):
            v = turn(acc[s, r, pl.ds(h * HEAD, HEAD)] * scale, c, n)
            rolled = pltpu.roll(v, HALF, 1)
            first = jnp.where(low, jnp.where(upper == 0, v, rolled), 0.0)
            second = jnp.where(low, jnp.where(upper == 0, rolled, v), 0.0)
            q_out[s, r, pl.ds(2 * h * HEAD, HEAD)] = first.astype(jnp.bfloat16)
            q_out[s, r, pl.ds((2 * h + 1) * HEAD, HEAD)] = second.astype(jnp.bfloat16)
        return 0

    lax.fori_loop(0, 8, queries, 0)
    swap.wait()
    kv_out[:, :, pl.ds(HEAD, HEAD)] = kv_other[...]
    side_end()
    keep.wait()
    for copy in started:
        copy.wait_send()


def project(emb, wq, wkv, gain, row_slot, needed, lengths, prefix_kv, w_out):
    groups, names = needed.shape
    steps, rows, width = emb.shape
    q_cols = wq.shape[1]
    heads = q_cols // HEAD
    vmem = pl.BlockSpec(memory_space=pltpu.VMEM)
    hbm = pl.BlockSpec(memory_space=pl.ANY)
    smem = pl.BlockSpec(memory_space=pltpu.SMEM)
    tp = RING * RING
    owned, longest, kv_width = prefix_kv.shape
    short = longest // 2
    depth, out_cols = w_out.shape
    return pl.pallas_call(
        project_kernel,
        out_shape=(
            jax.ShapeDtypeStruct((steps, rows, heads * 2 * HEAD), jnp.bfloat16),
            jax.ShapeDtypeStruct((steps, rows, 2 * HEAD), jnp.bfloat16),
            jax.ShapeDtypeStruct((2, groups, owned * 3 // 2, short, kv_width), jnp.bfloat16),
            jax.ShapeDtypeStruct(
                (groups, RING - 1, depth // groups, out_cols // RING), jnp.bfloat16
            ),
            jax.ShapeDtypeStruct((names,), jnp.int32),
        ),
        in_specs=[hbm, hbm, hbm, vmem, vmem, smem, smem, hbm, hbm, hbm],
        out_specs=(vmem, vmem, hbm, hbm, smem),
        scratch_shapes=[
            pltpu.VMEM((steps, tp, rows, width), jnp.bfloat16),
            pltpu.VMEM((tp * width, q_cols), jnp.bfloat16),
            pltpu.VMEM((tp * width, HEAD), jnp.bfloat16),
            pltpu.VMEM((steps, rows, q_cols + HEAD), jnp.float32),
            pltpu.VMEM((steps, rows, HEAD), jnp.float32),
            pltpu.VMEM((steps, rows, HEAD), jnp.float32),
            pltpu.VMEM((steps, rows, HEAD), jnp.float32),
            pltpu.VMEM((steps, rows, HEAD), jnp.bfloat16),
            pltpu.VMEM((owned * 3 // 2, short, kv_width), jnp.bfloat16),
            pltpu.VMEM((2, 2 * names, HEAD), jnp.float32),
            pltpu.SemaphoreType.DMA((5,)),
            pltpu.SemaphoreType.DMA((2,)),
            pltpu.SemaphoreType.DMA((2, RING + 1, 4)),
            pltpu.SemaphoreType.DMA((2, RING + 1, 4)),
            pltpu.SemaphoreType.DMA((2,)),
            pltpu.SemaphoreType.DMA((26,)),
            pltpu.SemaphoreType.DMA((26,)),
        ],
        compiler_params=pltpu.CompilerParams(
            collective_id=0, has_side_effects=True, vmem_limit_bytes=58 * MIB
        ),
        cost_estimate=pl.CostEstimate(
            flops=2 * steps * rows * tp * width * (q_cols + HEAD),
            bytes_accessed=300 * MIB,
            transcendentals=0,
        ),
        name="project",
    )(
        emb, wq, wkv, gain, row_slot, needed, lengths,
        prefix_kv.reshape(2 * owned, short, kv_width),
        prefix_kv.reshape(owned, 2, short, kv_width),
        w_out.reshape(groups, depth // groups, out_cols),
    )


def attend_kernel(
    begin, needed, lengths, q, own, cache, out,
    kv, later, items, kv_sem, owned,
):
    steps, rows = q.shape[0], q.shape[1]
    heads = q.shape[2] // (2 * HEAD)
    many = steps * heads * SUB
    slots, longest = kv.shape[0], kv.shape[1]
    short = longest // 2
    n_long = owned // 2
    g = lax.axis_index("grp")
    upper = lax.rem(lax.axis_index("tp"), 2)
    factor = math.log2(math.e) / math.sqrt(HEAD)
    nt = (((1,), (1,)), ((), ()))

    def length_of(slot):
        return lengths[needed[g, slot]]

    def fetch(slot, half, size):
        prefix = needed[g, slot]
        owner, local = lax.div(prefix, owned), lax.rem(prefix, owned)
        block = owner * (owned + n_long) + jnp.where(local < n_long, 2 * local, local + n_long)
        return pltpu.make_async_copy(
            cache.at[half, pl.ds(pl.multiple_of(block * short, short), size)],
            kv.at[slot, pl.ds(0, size), pl.ds(half * HEAD, HEAD)],
            kv_sem.at[slot, half],
        )

    def each(slot, do):
        for size in (short, longest):

            @pl.when((length_of(slot) > short) == (size == longest))
            def _():
                for half in (0, 1):
                    do(fetch(slot, half, size))

        return 0

    lax.fori_loop(0, slots, lambda n, _: each(n, lambda copy: copy.start()), 0)

    def plan(slot, counts):
        lo = begin[slot]
        hi = jnp.where(slot == slots - 1, rows, begin[jnp.minimum(slot + 1, slots - 1)])
        long = length_of(slot) > short

        def add(i, counts):
            n = jnp.where(long, counts[0], counts[1])
            items[jnp.where(long, 0, 1), n] = slot * rows + i
            return counts[0] + jnp.where(long, 1, 0), counts[1] + jnp.where(long, 0, 1)

        return lax.fori_loop(lax.div(lo, SUB), lax.div(hi + SUB - 1, SUB), add, counts)

    n_items = lax.fori_loop(0, slots, plan, (jnp.int32(0), jnp.int32(0)))
    row = lax.broadcasted_iota(jnp.int32, later.shape, 0)
    col = lax.broadcasted_iota(jnp.int32, later.shape, 1)
    allowed = (lax.rem(row, SUB) == lax.rem(col, SUB)) & (
        lax.div(col, SUB) <= lax.div(row, heads * SUB)
    )
    later[...] = jnp.where(allowed, 0.0, -jnp.inf)
    lax.fori_loop(0, slots, lambda n, _: each(n, lambda copy: copy.wait()), 0)

    def run(kind, size):
        def scores_of(item):
            slot, i = lax.div(item, rows), lax.rem(item, rows)
            r = pl.ds(pl.multiple_of(i * SUB, SUB), SUB)
            query = jnp.concatenate(
                [
                    q[s, r, pl.ds(h * 2 * HEAD, 2 * HEAD)]
                    for s in range(steps)
                    for h in range(heads)
                ],
                axis=0,
            )
            mine = jnp.concatenate([own[s, r, :] for s in range(steps)], axis=0)
            parts = [
                lax.dot_general(query, mine, nt, preferred_element_type=jnp.float32) + later[...]
            ]
            for first in range(0, size, short):
                keys = kv[slot, pl.ds(first, short), :]
                raw = lax.dot_general(query, keys, nt, preferred_element_type=jnp.float32)
                if first + short == size:
                    key = lax.broadcasted_iota(jnp.int32, (1, short), 1) + first
                    raw = raw + jnp.where(key < length_of(slot), 0.0, -jnp.inf)
                parts.append(raw)
            return slot, r, i, mine, parts

        def weights_of(parts):
            top = functools.reduce(
                jnp.maximum, [jnp.max(part, axis=1, keepdims=True) for part in parts]
            )
            weights, total = [], None
            for part in parts:
                weight = jnp.exp2((part - top) * factor)
                add = jnp.sum(weight, axis=1, keepdims=True)
                total = add if total is None else total + add
                weights.append(weight.astype(jnp.bfloat16))
            return weights, total

        def values_of(slot, mine, weights, total):
            summed = jnp.dot(weights[0], mine, preferred_element_type=jnp.float32)
            for n, weight in enumerate(weights[1:]):
                values = kv[slot, pl.ds(n * short, short), :]
                summed = summed + jnp.dot(weight, values, preferred_element_type=jnp.float32)
            summed = summed / total
            here, there = summed[:, :HEAD], summed[:, HEAD:]
            low = lax.broadcasted_iota(jnp.int32, here.shape, 1) < HALF
            first = jnp.where(upper == 0, here, there)
            second = jnp.where(upper == 0, there, here)
            return jnp.where(low, pltpu.roll(first, HALF, 1), second)

        def store(slot, r, i, result):
            lo = begin[slot]
            hi = jnp.where(slot == slots - 1, rows, begin[jnp.minimum(slot + 1, slots - 1)])
            at_row = lax.broadcasted_iota(jnp.int32, (SUB, HEAD), 0) + i * SUB
            inside = (at_row >= lo) & (at_row < hi)
            for s in range(steps):
                for h in range(heads):
                    j = (s * heads + h) * SUB
                    c = pl.ds(h * HEAD, HEAD)
                    before = out[s, r, c].astype(jnp.float32)
                    out[s, r, c] = jnp.where(inside, result[j : j + SUB], before).astype(
                        jnp.bfloat16
                    )

        def two(p, _):
            last = n_items[kind] - 1
            taken = [items[kind, jnp.minimum(2 * p + e, last)] for e in (0, 1)]
            scored = [scores_of(item) for item in taken]
            soft = [weights_of(parts) for *_, parts in scored]
            results = [
                values_of(slot, mine, *pair)
                for (slot, r, i, mine, _), pair in zip(scored, soft)
            ]
            for (slot, r, i, _, _), result in zip(scored, results):
                store(slot, r, i, result)
            return 0

        lax.fori_loop(0, lax.div(n_items[kind] + 1, 2), two, 0)

    run(0, longest)
    run(1, short)


def attend(begin, needed, lengths, q, own, cache, owned):
    steps, rows, wide = q.shape
    slots = needed.shape[1]
    short, kv_width = cache.shape[3:]
    cache = cache.reshape(2, -1, kv_width)
    vmem = pl.BlockSpec(memory_space=pltpu.VMEM)
    smem = pl.BlockSpec(memory_space=pltpu.SMEM)
    heads = wide // (2 * HEAD)
    return pl.pallas_call(
        functools.partial(attend_kernel, owned=owned),
        out_shape=jax.ShapeDtypeStruct((steps, rows, wide // 2), jnp.bfloat16),
        in_specs=[smem, smem, smem, vmem, vmem, pl.BlockSpec(memory_space=pl.ANY)],
        out_specs=vmem,
        scratch_shapes=[
            pltpu.VMEM((slots, 2 * short, 2 * kv_width), jnp.bfloat16),
            pltpu.VMEM((steps * heads * SUB, steps * SUB), jnp.float32),
            pltpu.SMEM((2, rows // SUB + slots), jnp.int32),
            pltpu.SemaphoreType.DMA((slots, 2)),
        ],
        compiler_params=pltpu.CompilerParams(vmem_limit_bytes=58 * MIB),
        cost_estimate=pl.CostEstimate(
            flops=8 * 10**9, bytes_accessed=60 * MIB, transcendentals=5 * 10**6
        ),
        name="attend",
    )(begin, needed, lengths, q, own, cache)


def output_kernel(
    a, wo_here, wo, emb, out, gathered, w, away, back, middle, total,
    load_sem, w_sem, ag_send, ag_recv, rs_send, rs_recv, sizes,
):
    depth, cols = a.shape[1], out.shape[1]
    t, x, z = place()
    quarter = wo.shape[3]
    firsts = [sum(sizes[:r]) for r in range(len(sizes))]
    ahead, behind = 1, RING - 1
    ways = (ahead, behind)
    started = []

    def go(copy):
        copy.start()
        started.append(copy)

    def whole(r):
        return pl.ds(firsts[r], sizes[r])

    def part(r, u):
        return pl.ds(firsts[r] + u * (sizes[r] // 2), sizes[r] // 2)

    def line(d):
        return {"tp": index_of(x + d, z)}

    def column(d):
        return {"tp": index_of(x, z + d)}

    def remote(src, dst, sends, recvs, device):
        return pltpu.make_async_remote_copy(
            src_ref=src,
            dst_ref=dst,
            send_sem=sends,
            recv_sem=recvs,
            device_id=device,
            device_id_type=MESH,
        )

    def share(r, d):
        i = 0 if d == ahead else 1
        return remote(
            gathered.at[0, whole(r)], gathered.at[d, whole(r)],
            ag_send.at[r, i], ag_recv.at[r, i], line(d),
        )

    def forward(r, u):
        return remote(
            gathered.at[ways[u], part(r, u)], gathered.at[2, part(r, u)],
            ag_send.at[r, 2 + u], ag_recv.at[r, 2 + u], line(ways[u]),
        )

    def give(r, n, u):
        return remote(
            away.at[n, part(r, u)], back.at[n, part(r, u)],
            rs_send.at[r, 2 * n + u], rs_recv.at[r, 2 * n + u],
            column(ways[u] if n < 2 else ways[1 - u]),
        )

    def offer(r):
        for d in ways:
            go(share(r, d))

    def arrive(r):
        for u in (0, 1):
            share(r, ways[u]).wait_recv()
            go(forward(r, u))

    def product(r, d):
        c = pl.ds(pl.multiple_of(lax.rem(z + d, RING) * cols, cols), cols)
        result = None
        for k in range(RING):
            term = jnp.dot(
                gathered[k, whole(r), :],
                w[k, :, :, c].reshape(depth, cols),
                preferred_element_type=jnp.float32,
            )
            result = term if result is None else result + term
        return result

    def far(r):
        for u in (0, 1):
            forward(r, u).wait_recv()
        away[0, whole(r), :] = product(r, 2).astype(jnp.bfloat16)
        for u in (0, 1):
            go(give(r, 0, u))

    def near(r):
        n = sizes[r] // 2
        for u in (0, 1):
            value = product(r, ways[u])
            straight = value[n:] if u == 0 else value[:n]
            passing = value[:n] if u == 0 else value[n:]
            away[2, part(r, 1 - u), :] = straight.astype(jnp.bfloat16)
            go(give(r, 2, 1 - u))
            middle[part(r, u), :] = passing

    def mine(r):
        total[whole(r), :] = product(r, 0) + emb[whole(r), :].astype(jnp.float32)

    def relay(r):
        for u in (0, 1):
            give(r, 0, u).wait_recv()
            value = middle[part(r, u), :] + back[0, part(r, u), :].astype(jnp.float32)
            away[1, part(r, u), :] = value.astype(jnp.bfloat16)
            go(give(r, 1, u))

    def finish(r):
        for n in (2, 1):
            for u in (0, 1):
                give(r, n, u).wait_recv()
        value = total[whole(r), :]
        for n in (2, 1):
            value = value + back[n, whole(r), :].astype(jnp.float32)
        out[whole(r), :] = value.astype(jnp.bfloat16)

    greet(around(x, z))
    load = pltpu.make_async_copy(a, gathered.at[0], load_sem)
    load.start()
    load.wait()
    c = pl.ds(pl.multiple_of(x * quarter, quarter), quarter)
    weights = [pltpu.make_async_copy(wo_here.at[:, :, c], w.at[0], w_sem.at[0])] + [
        pltpu.make_async_copy(wo.at[:, k - 1], w.at[k], w_sem.at[k]) for k in range(1, RING)
    ]
    offer(0)
    offer(1)
    for copy in weights:
        copy.start()
    arrive(0)
    offer(2)
    for copy in weights:
        copy.wait()
    count = len(sizes)
    for r in range(count):
        if r + 1 < count:
            arrive(r + 1)
        far(r)
        if r + 3 < count:
            offer(r + 3)
        near(r)
        if r:
            relay(r - 1)
        mine(r)
        if r > 1:
            finish(r - 2)
    relay(count - 1)
    for r in (count - 2, count - 1):
        finish(r)
    for copy in started:
        copy.wait_send()


def output(a, w_out, wo, emb, sizes):
    rows, depth = a.shape
    cols = emb.shape[1]
    chunks = len(sizes)
    vmem = pl.BlockSpec(memory_space=pltpu.VMEM)
    hbm = pl.BlockSpec(memory_space=pl.ANY)
    dma = pltpu.SemaphoreType.DMA
    return pl.pallas_call(
        functools.partial(output_kernel, sizes=sizes),
        out_shape=jax.ShapeDtypeStruct((rows, cols), jnp.bfloat16),
        in_specs=[hbm, hbm, hbm, vmem],
        out_specs=vmem,
        scratch_shapes=[
            pltpu.VMEM((RING, rows, depth), jnp.bfloat16),
            pltpu.VMEM((RING,) + wo.shape[:1] + wo.shape[2:], jnp.bfloat16),
            pltpu.VMEM((3, rows, cols), jnp.bfloat16),
            pltpu.VMEM((3, rows, cols), jnp.bfloat16),
            pltpu.VMEM((rows, cols), jnp.float32),
            pltpu.VMEM((rows, cols), jnp.float32),
            dma,
            dma((RING,)),
            dma((chunks, 4)),
            dma((chunks, 4)),
            dma((chunks, 6)),
            dma((chunks, 6)),
        ],
        compiler_params=pltpu.CompilerParams(
            collective_id=1, has_side_effects=True, vmem_limit_bytes=58 * MIB
        ),
        cost_estimate=pl.CostEstimate(
            flops=2 * rows * depth * RING * RING * cols, bytes_accessed=150 * MIB, transcendentals=0
        ),
        name="output",
    )(a, w_out.reshape(wo.shape[0], wo.shape[2], w_out.shape[1]), wo, emb)


def body(embedded, norm_gain, w_query, w_keyval, w_out, prefix_kv, prefix_len, needed, row_slot):
    steps, rows, width = embedded.shape
    q, own, cache, wo, begin = project(
        embedded, w_query, w_keyval, norm_gain[None], row_slot, needed, prefix_len, prefix_kv, w_out
    )
    attended = attend(begin, needed, prefix_len, q, own, cache, prefix_kv.shape[0])
    mixed = output(
        attended.reshape(steps * rows, width),
        w_out,
        wo,
        embedded.reshape(steps * rows, width),
        (128, 256, 256, 256, 128),
    )
    return mixed.reshape(steps, rows, width)


def solution(mesh):
    in_specs = (
        P(None, "grp", "tp"),
        P(),
        P(None, "tp"),
        P(None, "tp"),
        P("tp", None),
        P("grp", None, "tp"),
        P(),
        P(),
        P("grp", None),
    )
    out_specs = P(None, "grp", "tp")
    return jax.shard_map(body, mesh=mesh, in_specs=in_specs, out_specs=out_specs, check_vma=False)
```

```python
import functools
import math

import jax
import jax.numpy as jnp
from jax import lax
from jax.experimental import pallas as pl
from jax.experimental.pallas import tpu as pltpu
from jax.sharding import PartitionSpec as P

HEAD = 128
HALF = 64
RING = 4
EPSILON = 1e-05
ROPE_THETA = 500000.0
SUB = 32
FIRST_ROWS = 544
MIB = 1 << 20
MESH = pl.DeviceIdType.MESH
ORDER = (0, 3, 1, 2)


def place():
    t = lax.axis_index("tp")
    return t, lax.div(t, RING), lax.rem(t, RING)


def index_of(x, z):
    return lax.rem(x, RING) * RING + lax.rem(z, RING)


def greet(partners):
    barrier = pltpu.get_barrier_semaphore()
    for device in partners:
        pl.semaphore_signal(barrier, inc=1, device_id=device, device_id_type=MESH)
    pl.semaphore_wait(barrier, len(partners))


def around(x, z):
    return [{"tp": index_of(x + a, z + b)} for a, b in ((1, 0), (3, 0), (0, 1), (0, 3))]


def project_kernel(
    emb, wq, wkv, gain, row_slot, needed, lengths, prefix, prefix_halves, wo_here,
    q_out, kv_out, cache, wo, begin,
    blocks_a, blocks_b, w_q, w_kv, acc, squares, cosine, sine, kv_other, mine, table,
    load_sem, w_sem, send_sem, recv_sem, kv_sem, side_send, side_recv,
):
    all_rows, width = emb.shape
    rows = all_rows // 2
    q_cols = wq.shape[1]
    t, x, z = place()
    blocks = (blocks_a, blocks_b)
    halves = tuple(ref.shape[1] // 2 for ref in blocks)
    firsts = (0, 2 * halves[0])

    def slot_of(s, along, across):
        return index_of(x + across, z + along) if s == 0 else index_of(x + along, z + across)

    def neighbour(s, phase, d):
        on_z = (s == 0) == (phase == 0)
        return {"tp": index_of(x, z + d) if on_z else index_of(x + d, z)}

    def move(s, phase, o, kind, slot, d):
        ref = blocks[s].at[slot]
        if kind == 2:
            ref = blocks[s].at[slot, pl.ds(0, halves[s])]
        if kind == 3:
            ref = blocks[s].at[slot, pl.ds(halves[s], halves[s])]
        i = o if phase else RING
        return pltpu.make_async_remote_copy(
            src_ref=ref,
            dst_ref=ref,
            send_sem=send_sem.at[s, i, kind],
            recv_sem=recv_sem.at[s, i, kind],
            device_id=neighbour(s, phase, d),
            device_id_type=MESH,
        )

    def at(s, phase, o, far):
        return slot_of(s, far, 0) if phase == 0 else slot_of(s, ORDER[o], far)

    started = []

    def start(*a):
        copy = move(*a)
        copy.start()
        started.append(copy)

    def send(s, phase, o):
        slot = at(s, phase, o, 0)
        start(s, phase, o, 0, slot, 1)
        start(s, phase, o, 1, slot, RING - 1)

    def pass_on(s, phase, o):
        back, ahead = at(s, phase, o, 3), at(s, phase, o, 1)
        move(s, phase, o, 0, back, 1).wait_recv()
        start(s, phase, o, 2, back, 1)
        move(s, phase, o, 1, ahead, 1).wait_recv()
        start(s, phase, o, 3, ahead, RING - 1)

    def opposite(s, phase, o):
        slot = at(s, phase, o, 2)
        move(s, phase, o, 2, slot, 1).wait_recv()
        move(s, phase, o, 3, slot, 1).wait_recv()

    def multiply(*todo):
        for s in (0, 1):
            slots = [slot for other, slot in todo if other == s]
            if slots:
                accumulate(s, slots)

    def accumulate(s, slots):
        half = halves[s]

        def one(i, _):
            which, lower = lax.div(i, 2), lax.rem(i, 2)
            slot = slots[0]
            for j in range(1, len(slots)):
                slot = jnp.where(which == j, slots[j], slot)
            value = blocks[s][slot, pl.ds(pl.multiple_of(lower * half, 16), half), :]
            value = value.astype(jnp.float32)
            r = pl.ds(pl.multiple_of(firsts[s] + lower * half, 16), half)
            square = value * value
            total = square[:, :128]
            for c in range(1, width // 128):
                total = total + square[:, c * 128 : (c + 1) * 128]
            squares[r, :] += total
            depth = pl.ds(pl.multiple_of(slot * width, width), width)
            scaled = (value * gain[:, depth]).astype(jnp.bfloat16)
            for ref, c in ((w_q, pl.ds(0, q_cols)), (w_kv, pl.ds(q_cols, HEAD))):
                acc[r, c] += jnp.dot(scaled, ref[depth, :], preferred_element_type=jnp.float32)
            return 0

        lax.fori_loop(0, 2 * len(slots), one, 0)

    g = lax.axis_index("grp")
    y, core = lax.div(g, 2), lax.rem(g, 2)
    upper = lax.rem(t, 2)
    n_short = prefix_halves.shape[0] // 2
    n_long = 2 * n_short
    piece = wo.shape[2]
    quarter = wo.shape[3]
    cut = piece // 2
    other_half = {"tp": t + 1 - 2 * upper}
    sibling = {"grp": g + 1 - 2 * core}

    def group(a, flip=False):
        return lax.rem(y + a, RING) * 2 + (1 - core if flip else core)

    def up(d):
        return {"grp": group(d)}

    def side(n, src, dst, device):
        return pltpu.make_async_remote_copy(
            src_ref=src,
            dst_ref=dst,
            send_sem=side_send.at[n],
            recv_sem=side_recv.at[n],
            device_id=device,
            device_id_type=MESH,
        )

    def go(copy):
        copy.start()
        started.append(copy)

    def pair():
        return side(0, mine, cache.at[1, g], other_half)

    def cache_ring(h, d, group_id):
        ref = cache.at[h, group_id]
        return side(1 + 2 * h + (0 if d == 1 else 1), ref if h else mine, ref, up(d))

    def cache_forward(h, group_id):
        ref = cache.at[h, group_id]
        return side(5 + h, ref, ref, up(1 if h == 0 else RING - 1))

    def cache_sibling(h, a, flip=False):
        ref = cache.at[h, group(a, flip)]
        return side(7 + 4 * h + a, ref if h or a else mine, ref, sibling)

    def wo_line(k):
        c = pl.ds(pl.multiple_of(lax.rem(x + k, RING) * quarter, quarter), quarter)
        return side(
            14 + k, wo_here.at[g, :, c], wo.at[g, k - 1], {"tp": index_of(x + k, z)}
        )

    def wo_ring(d, group_id):
        ref = wo.at[group_id]
        return side(18 if d == 1 else 19, ref, ref, up(d))

    def wo_forward(d, group_id):
        ref = wo.at[group_id, :, pl.ds(0 if d == 1 else cut, cut)]
        return side(20 if d == 1 else 21, ref, ref, up(d))

    def wo_sibling(a, flip=False):
        ref = wo.at[group(a, flip)]
        return side(22 + a, ref, ref, sibling)

    ahead, back = 1, RING - 1

    def side_begin():
        go(pair())
        for d in (ahead, back):
            go(cache_ring(0, d, g))
        for k in (1, 2, 3):
            go(wo_line(k))

    def side_line():
        for k in (1, 2, 3):
            wo_line(k).wait_recv()
        for d in (ahead, back):
            go(wo_ring(d, g))
        go(wo_sibling(0))

    def side_pair():
        pair().wait_recv()
        for d in (ahead, back):
            go(cache_ring(1, d, g))
        for h in (0, 1):
            go(cache_sibling(h, 0))

    def side_cache(h):
        cache_ring(h, ahead, group(back)).wait_recv()
        if h == 0:
            go(cache_forward(h, group(back)))
        cache_ring(h, back, group(ahead)).wait_recv()
        if h == 1:
            go(cache_forward(h, group(ahead)))
        go(cache_sibling(h, back))
        go(cache_sibling(h, ahead))

    def side_wo():
        wo_ring(ahead, group(back)).wait_recv()
        go(wo_forward(ahead, group(back)))
        wo_ring(back, group(ahead)).wait_recv()
        go(wo_forward(back, group(ahead)))
        go(wo_sibling(back))
        go(wo_sibling(ahead))

    def side_cache_far(h):
        cache_forward(h, group(2)).wait_recv()
        go(cache_sibling(h, 2))

    def side_wo_far():
        wo_forward(ahead, group(2)).wait_recv()
        wo_forward(back, group(2)).wait_recv()
        go(wo_sibling(2))

    def side_end():
        for a in range(RING):
            for h in (0, 1):
                cache_sibling(h, a, True).wait_recv()
            wo_sibling(a, True).wait_recv()

    loads = [
        pltpu.make_async_copy(
            emb.at[pl.ds(firsts[s], 2 * halves[s])], blocks[s].at[t], load_sem.at[s]
        )
        for s in (0, 1)
    ]
    own_cache = [
        pltpu.make_async_copy(
            prefix.at[pl.ds(0, n_long)], mine.at[pl.ds(0, n_long)], load_sem.at[2]
        ),
        pltpu.make_async_copy(
            prefix_halves.at[pl.ds(n_short, n_short), 0],
            mine.at[pl.ds(n_long, n_short)],
            load_sem.at[3],
        ),
    ]
    weights = [
        pltpu.make_async_copy(wq, w_q, w_sem.at[0]),
        pltpu.make_async_copy(wkv, w_kv, w_sem.at[1]),
    ]
    for copy in loads + own_cache:
        copy.start()
    greet(
        around(x, z)
        + [{"tp": index_of(x + 2, z)}, sibling, up(ahead), up(back)]
    )
    for copy in loads:
        copy.wait()
    for copy in own_cache:
        copy.wait()
    side_begin()
    for s in (0, 1):
        send(s, 0, 0)
    keep = pltpu.make_async_copy(mine, cache.at[0, g], load_sem.at[4])
    keep.start()
    for copy in weights:
        copy.start()
    for s in (0, 1):
        send(s, 1, 0)
    acc[...] = jnp.zeros_like(acc)
    squares[...] = jnp.zeros_like(squares)

    names = table.shape[1] // 2
    line = lax.broadcasted_iota(jnp.int32, (2 * names, HEAD), 0)
    lane = lax.broadcasted_iota(jnp.int32, (2 * names, HEAD), 1)
    position = jnp.zeros((2 * names, HEAD), jnp.int32)
    starts = []
    for n in range(names):
        length = lengths[needed[g, n]]
        position = jnp.where(line == n, length, position)
        position = jnp.where(line == names + n, length + 1, position)
        starts.append(jnp.sum(jnp.where(row_slot[...] < n, 1, 0)))
        begin[n] = starts[n]
    pair_index = lax.div(lane, 2).astype(jnp.float32)
    inverse = jnp.exp(pair_index * (-2.0 * math.log(ROPE_THETA) / HEAD))
    angle = position.astype(jnp.float32) * inverse
    table[0] = jnp.cos(angle)
    table[1] = jnp.sin(angle) * jnp.where(lax.rem(lane, 2) == 0, -1.0, 1.0)

    def spread(i, _):
        s = lax.div(i * 128, rows)
        row = lax.broadcasted_iota(jnp.int32, (128, HEAD), 0) + lax.rem(i * 128, rows)
        for k, ref in ((0, cosine), (1, sine)):
            out = jnp.zeros((128, HEAD), jnp.float32)
            for n in range(names):
                out = jnp.where(row >= starts[n], table[k, pl.ds(s * names + n, 1), :], out)
            ref[pl.ds(pl.multiple_of(i * 128, 128), 128), :] = out
        return 0

    lax.fori_loop(0, all_rows // 128, spread, 0)
    for copy in weights:
        copy.wait()
    both = (0, 1)
    multiply((0, t), (1, t))
    side_line()
    side_cache(0)
    for s in both:
        pass_on(s, 0, 0)
    for o in (1, 2):
        for s in both:
            send(s, 1, o)
    multiply(*[(s, at(s, 0, 0, d)) for d in (3, 1) for s in both])
    side_pair()
    for s in both:
        pass_on(s, 1, 0)
    multiply(*[(s, at(s, 1, 0, d)) for d in (3, 1) for s in both])
    for s in both:
        opposite(s, 0, 0)
        send(s, 1, 3)
    multiply(*[(s, at(s, 0, 0, 2)) for s in both])
    side_wo()
    for o in (1, 2, 3):
        for s in both:
            pass_on(s, 1, o)
        multiply(*[(s, at(s, 1, o, d)) for d in (3, 1) for s in both])
        if o == 1:
            side_cache(1)
        if o == 2:
            side_cache_far(0)
            side_wo_far()
        if o == 3:
            side_cache_far(1)
        for s in both:
            opposite(s, 1, o - 1)
        multiply(*[(s, at(s, 1, o - 1, 2)) for s in both])
    def turn(v, c, n):
        even = lax.rem(lax.broadcasted_iota(jnp.int32, v.shape, 1), 2) == 0
        other = jnp.where(even, pltpu.roll(v, HEAD - 1, 1), pltpu.roll(v, 1, 1))
        return v * c + other * n

    def scale_of(r):
        mean = jnp.sum(squares[r, :], axis=1, keepdims=True) / (RING * RING * width)
        return lax.rsqrt(mean + EPSILON)

    def tile(s, i):
        return pl.ds(pl.multiple_of(firsts[s] + i * halves[s], 16), halves[s])

    def own_kv(s):
        def one(i, _):
            r = tile(s, i)
            v = acc[r, pl.ds(q_cols, HEAD)] * scale_of(r)
            c, n = cosine[r, :], sine[r, :]
            low = lax.broadcasted_iota(jnp.int32, v.shape, 1) < HALF
            c = jnp.where(upper == 0, c, pltpu.roll(c, HALF, 1))
            n = jnp.where(upper == 0, n, pltpu.roll(n, HALF, 1))
            kv_out[r, pl.ds(0, HEAD)] = jnp.where(low, turn(v, c, n), v).astype(jnp.bfloat16)
            return 0

        lax.fori_loop(0, 2, one, 0)

    def swap(s):
        r = pl.ds(firsts[s], 2 * halves[s])
        return pltpu.make_async_remote_copy(
            src_ref=kv_out.at[r, pl.ds(0, HEAD)],
            dst_ref=kv_other.at[r],
            send_sem=kv_sem.at[0, s],
            recv_sem=kv_sem.at[1, s],
            device_id=other_half,
            device_id_type=MESH,
        )

    def queries(s):
        def one(i, _):
            r = tile(s, i)
            scale = scale_of(r)
            c, n = cosine[r, :], sine[r, :]
            low = lax.broadcasted_iota(jnp.int32, c.shape, 1) < HALF
            for h in range(q_cols // HEAD):
                v = turn(acc[r, pl.ds(h * HEAD, HEAD)] * scale, c, n)
                rolled = pltpu.roll(v, HALF, 1)
                first = jnp.where(low, jnp.where(upper == 0, v, rolled), 0.0)
                second = jnp.where(low, jnp.where(upper == 0, rolled, v), 0.0)
                q_out[r, pl.ds(2 * h * HEAD, HEAD)] = first.astype(jnp.bfloat16)
                q_out[r, pl.ds((2 * h + 1) * HEAD, HEAD)] = second.astype(jnp.bfloat16)
            return 0

        lax.fori_loop(0, 2, one, 0)

    for s in both:
        opposite(s, 1, 3)
        multiply((s, at(s, 1, 3, 2)))
        own_kv(s)
        swap(s).start()
        queries(s)
    for s in both:
        swap(s).wait()
    kv_out[:, pl.ds(HEAD, HEAD)] = kv_other[...]
    side_end()
    keep.wait()
    for copy in started:
        copy.wait_send()


def project(emb, wq, wkv, gain, row_slot, needed, lengths, prefix_kv, w_out):
    groups, names = needed.shape
    steps, rows, width = emb.shape
    all_rows = steps * rows
    q_cols = wq.shape[1]
    heads = q_cols // HEAD
    vmem = pl.BlockSpec(memory_space=pltpu.VMEM)
    hbm = pl.BlockSpec(memory_space=pl.ANY)
    smem = pl.BlockSpec(memory_space=pltpu.SMEM)
    tp = RING * RING
    owned, longest, kv_width = prefix_kv.shape
    short = longest // 2
    depth, out_cols = w_out.shape
    return pl.pallas_call(
        project_kernel,
        out_shape=(
            jax.ShapeDtypeStruct((all_rows, heads * 2 * HEAD), jnp.bfloat16),
            jax.ShapeDtypeStruct((all_rows, 2 * HEAD), jnp.bfloat16),
            jax.ShapeDtypeStruct((2, groups, owned * 3 // 2, short, kv_width), jnp.bfloat16),
            jax.ShapeDtypeStruct(
                (groups, RING - 1, depth // groups, out_cols // RING), jnp.bfloat16
            ),
            jax.ShapeDtypeStruct((names,), jnp.int32),
        ),
        in_specs=[hbm, hbm, hbm, vmem, vmem, smem, smem, hbm, hbm, hbm],
        out_specs=(vmem, vmem, hbm, hbm, smem),
        scratch_shapes=[
            pltpu.VMEM((tp, FIRST_ROWS, width), jnp.bfloat16),
            pltpu.VMEM((tp, all_rows - FIRST_ROWS, width), jnp.bfloat16),
            pltpu.VMEM((tp * width, q_cols), jnp.bfloat16),
            pltpu.VMEM((tp * width, HEAD), jnp.bfloat16),
            pltpu.VMEM((all_rows, q_cols + HEAD), jnp.float32),
            pltpu.VMEM((all_rows, HEAD), jnp.float32),
            pltpu.VMEM((all_rows, HEAD), jnp.float32),
            pltpu.VMEM((all_rows, HEAD), jnp.float32),
            pltpu.VMEM((all_rows, HEAD), jnp.bfloat16),
            pltpu.VMEM((owned * 3 // 2, short, kv_width), jnp.bfloat16),
            pltpu.VMEM((2, 2 * names, HEAD), jnp.float32),
            pltpu.SemaphoreType.DMA((5,)),
            pltpu.SemaphoreType.DMA((2,)),
            pltpu.SemaphoreType.DMA((2, RING + 1, 4)),
            pltpu.SemaphoreType.DMA((2, RING + 1, 4)),
            pltpu.SemaphoreType.DMA((2, 2)),
            pltpu.SemaphoreType.DMA((26,)),
            pltpu.SemaphoreType.DMA((26,)),
        ],
        compiler_params=pltpu.CompilerParams(
            collective_id=0, has_side_effects=True, vmem_limit_bytes=58 * MIB
        ),
        cost_estimate=pl.CostEstimate(
            flops=2 * steps * rows * tp * width * (q_cols + HEAD),
            bytes_accessed=300 * MIB,
            transcendentals=0,
        ),
        name="project",
    )(
        emb.reshape(all_rows, width), wq, wkv, gain, row_slot, needed, lengths,
        prefix_kv.reshape(2 * owned, short, kv_width),
        prefix_kv.reshape(owned, 2, short, kv_width),
        w_out.reshape(groups, depth // groups, out_cols),
    )


def attend_kernel(
    begin, needed, lengths, q, own, cache, out,
    kv, later, items, scores, weights, kv_sem, owned,
):
    steps, rows = q.shape[0], q.shape[1]
    heads = q.shape[2] // (2 * HEAD)
    many = steps * heads * SUB
    slots, longest = kv.shape[0], kv.shape[1]
    short = longest // 2
    n_long = owned // 2
    g = lax.axis_index("grp")
    upper = lax.rem(lax.axis_index("tp"), 2)
    factor = math.log2(math.e) / math.sqrt(HEAD)
    nt = (((1,), (1,)), ((), ()))

    def length_of(slot):
        return lengths[needed[g, slot]]

    def fetch(slot, half, size):
        prefix = needed[g, slot]
        owner, local = lax.div(prefix, owned), lax.rem(prefix, owned)
        block = owner * (owned + n_long) + jnp.where(local < n_long, 2 * local, local + n_long)
        return pltpu.make_async_copy(
            cache.at[half, pl.ds(pl.multiple_of(block * short, short), size)],
            kv.at[slot, pl.ds(0, size), pl.ds(half * HEAD, HEAD)],
            kv_sem.at[slot, half],
        )

    def each(slot, do):
        for size in (short, longest):

            @pl.when((length_of(slot) > short) == (size == longest))
            def _():
                for half in (0, 1):
                    do(fetch(slot, half, size))

        return 0

    lax.fori_loop(0, slots, lambda n, _: each(n, lambda copy: copy.start()), 0)

    def plan(slot, counts):
        lo = begin[slot]
        hi = jnp.where(slot == slots - 1, rows, begin[jnp.minimum(slot + 1, slots - 1)])
        long = length_of(slot) > short

        def add(i, counts):
            n = jnp.where(long, counts[0], counts[1])
            items[jnp.where(long, 0, 1), n] = slot * rows + i
            return counts[0] + jnp.where(long, 1, 0), counts[1] + jnp.where(long, 0, 1)

        return lax.fori_loop(lax.div(lo, SUB), lax.div(hi + SUB - 1, SUB), add, counts)

    n_items = lax.fori_loop(0, slots, plan, (jnp.int32(0), jnp.int32(0)))
    row = lax.broadcasted_iota(jnp.int32, later.shape, 0)
    col = lax.broadcasted_iota(jnp.int32, later.shape, 1)
    allowed = (
        (lax.rem(row, SUB) == lax.rem(col, SUB))
        & (lax.div(col, SUB) <= lax.div(row, heads * SUB))
        & (col < steps * SUB)
    )
    later[...] = jnp.where(allowed, 0.0, -jnp.inf)
    lax.fori_loop(0, slots, lambda n, _: each(n, lambda copy: copy.wait()), 0)

    def run(kind, size):
        def scores_of(e, item):
            slot, i = lax.div(item, rows), lax.rem(item, rows)
            r = pl.ds(pl.multiple_of(i * SUB, SUB), SUB)
            query = jnp.concatenate(
                [
                    q[s, r, pl.ds(h * 2 * HEAD, 2 * HEAD)]
                    for s in range(steps)
                    for h in range(heads)
                ],
                axis=0,
            )
            mine = jnp.concatenate(
                [own[s, r, :] for s in range(steps)]
                + [jnp.zeros((HEAD - steps * SUB, 2 * HEAD), jnp.bfloat16)],
                axis=0,
            )
            scores[e, :, pl.ds(longest, HEAD)] = lax.dot_general(
                query, mine, nt, preferred_element_type=jnp.float32
            )
            for first in range(0, size, short):
                keys = kv[slot, pl.ds(first, short), :]
                scores[e, :, pl.ds(first, short)] = lax.dot_general(
                    query, keys, nt, preferred_element_type=jnp.float32
                )
            return slot, r, i, mine

        def weigh(e, slot):
            key = lax.broadcasted_iota(jnp.int32, (1, short), 1) + (size - short)
            last = jnp.where(key < length_of(slot), 0.0, -jnp.inf)
            totals = []
            for m in range(0, many, SUB):
                rows_here = pl.ds(m, SUB)
                tiles = []
                for first in range(0, size, HEAD):
                    tile = scores[e, rows_here, pl.ds(first, HEAD)]
                    if first >= size - short:
                        c = first - (size - short)
                        tile = tile + last[:, c : c + HEAD]
                    tiles.append(tile)
                tiles.append(scores[e, rows_here, pl.ds(longest, HEAD)] + later[rows_here, :])
                top = jnp.max(functools.reduce(jnp.maximum, tiles), axis=1, keepdims=True)
                tiles = [jnp.exp2((tile - top) * factor) for tile in tiles]
                total = jnp.sum(functools.reduce(jnp.add, tiles), axis=1, keepdims=True)
                totals.append(total)
                for n, tile in enumerate(tiles):
                    c = n * HEAD if n < size // HEAD else longest
                    weights[e, rows_here, pl.ds(c, HEAD)] = tile.astype(jnp.bfloat16)
            return totals

        def values_of(e, slot, mine, totals):
            summed = jnp.dot(
                weights[e, :, pl.ds(longest, HEAD)], mine, preferred_element_type=jnp.float32
            )
            summed = summed + jnp.dot(
                weights[e, :, pl.ds(0, size)],
                kv[slot, pl.ds(0, size), :],
                preferred_element_type=jnp.float32,
            )
            out_blocks = []
            for n, total in enumerate(totals):
                block = summed[n * SUB : (n + 1) * SUB] / total
                here, there = block[:, :HEAD], block[:, HEAD:]
                low = lax.broadcasted_iota(jnp.int32, here.shape, 1) < HALF
                first = jnp.where(upper == 0, here, there)
                second = jnp.where(upper == 0, there, here)
                out_blocks.append(jnp.where(low, pltpu.roll(first, HALF, 1), second))
            return out_blocks

        def store(slot, r, i, result):
            lo = begin[slot]
            hi = jnp.where(slot == slots - 1, rows, begin[jnp.minimum(slot + 1, slots - 1)])
            at_row = lax.broadcasted_iota(jnp.int32, (SUB, HEAD), 0) + i * SUB
            inside = (at_row >= lo) & (at_row < hi)
            for s in range(steps):
                for h in range(heads):
                    c = pl.ds(h * HEAD, HEAD)
                    before = out[s, r, c].astype(jnp.float32)
                    out[s, r, c] = jnp.where(inside, result[s * heads + h], before).astype(
                        jnp.bfloat16
                    )

        def two(p, _):
            last = n_items[kind] - 1
            taken = [items[kind, jnp.minimum(2 * p + e, last)] for e in (0, 1)]
            scored = [scores_of(e, taken[e]) for e in (0, 1)]
            totals = [weigh(e, scored[e][0]) for e in (0, 1)]
            results = [values_of(e, scored[e][0], scored[e][3], totals[e]) for e in (0, 1)]
            for (slot, r, i, _), result in zip(scored, results):
                store(slot, r, i, result)
            return 0

        lax.fori_loop(0, lax.div(n_items[kind] + 1, 2), two, 0)

    run(0, longest)
    run(1, short)


def attend(begin, needed, lengths, q, own, cache, owned):
    steps, rows, wide = q.shape
    slots = needed.shape[1]
    short, kv_width = cache.shape[3:]
    cache = cache.reshape(2, -1, kv_width)
    vmem = pl.BlockSpec(memory_space=pltpu.VMEM)
    smem = pl.BlockSpec(memory_space=pltpu.SMEM)
    heads = wide // (2 * HEAD)
    return pl.pallas_call(
        functools.partial(attend_kernel, owned=owned),
        out_shape=jax.ShapeDtypeStruct((steps, rows, wide // 2), jnp.bfloat16),
        in_specs=[smem, smem, smem, vmem, vmem, pl.BlockSpec(memory_space=pl.ANY)],
        out_specs=vmem,
        scratch_shapes=[
            pltpu.VMEM((slots, 2 * short, 2 * kv_width), jnp.bfloat16),
            pltpu.VMEM((steps * heads * SUB, HEAD), jnp.float32),
            pltpu.SMEM((2, rows // SUB + slots), jnp.int32),
            pltpu.VMEM((2, steps * heads * SUB, 2 * short + HEAD), jnp.float32),
            pltpu.VMEM((2, steps * heads * SUB, 2 * short + HEAD), jnp.bfloat16),
            pltpu.SemaphoreType.DMA((slots, 2)),
        ],
        compiler_params=pltpu.CompilerParams(vmem_limit_bytes=58 * MIB),
        cost_estimate=pl.CostEstimate(
            flops=8 * 10**9, bytes_accessed=60 * MIB, transcendentals=5 * 10**6
        ),
        name="attend",
    )(begin, needed, lengths, q, own, cache)


def output_kernel(
    a, wo_here, wo, emb, out, gathered, w, away, back, middle, total,
    load_sem, w_sem, ag_send, ag_recv, rs_send, rs_recv, sizes,
):
    depth, cols = a.shape[1], out.shape[1]
    t, x, z = place()
    quarter = wo.shape[3]
    firsts = [sum(sizes[:r]) for r in range(len(sizes))]
    ahead, behind = 1, RING - 1
    ways = (ahead, behind)
    started = []

    def go(copy):
        copy.start()
        started.append(copy)

    def whole(r):
        return pl.ds(firsts[r], sizes[r])

    def part(r, u):
        return pl.ds(firsts[r] + u * (sizes[r] // 2), sizes[r] // 2)

    def line(d):
        return {"tp": index_of(x + d, z)}

    def column(d):
        return {"tp": index_of(x, z + d)}

    def remote(src, dst, sends, recvs, device):
        return pltpu.make_async_remote_copy(
            src_ref=src,
            dst_ref=dst,
            send_sem=sends,
            recv_sem=recvs,
            device_id=device,
            device_id_type=MESH,
        )

    def share(r, d):
        i = 0 if d == ahead else 1
        return remote(
            gathered.at[0, whole(r)], gathered.at[d, whole(r)],
            ag_send.at[r, i], ag_recv.at[r, i], line(d),
        )

    def forward(r, u):
        return remote(
            gathered.at[ways[u], part(r, u)], gathered.at[2, part(r, u)],
            ag_send.at[r, 2 + u], ag_recv.at[r, 2 + u], line(ways[u]),
        )

    def give(r, n, u):
        return remote(
            away.at[n, part(r, u)], back.at[n, part(r, u)],
            rs_send.at[r, 2 * n + u], rs_recv.at[r, 2 * n + u],
            column(ways[u] if n < 2 else ways[1 - u]),
        )

    def offer(r):
        for d in ways:
            go(share(r, d))

    def arrive(r):
        for u in (0, 1):
            share(r, ways[u]).wait_recv()
            go(forward(r, u))

    def product(r, d):
        c = pl.ds(pl.multiple_of(lax.rem(z + d, RING) * cols, cols), cols)
        result = None
        for k in range(RING):
            term = jnp.dot(
                gathered[k, whole(r), :],
                w[k, :, :, c].reshape(depth, cols),
                preferred_element_type=jnp.float32,
            )
            result = term if result is None else result + term
        return result

    def far(r):
        for u in (0, 1):
            forward(r, u).wait_recv()
        away[0, whole(r), :] = product(r, 2).astype(jnp.bfloat16)
        for u in (0, 1):
            go(give(r, 0, u))

    def near(r):
        n = sizes[r] // 2
        for u in (0, 1):
            value = product(r, ways[u])
            straight = value[n:] if u == 0 else value[:n]
            passing = value[:n] if u == 0 else value[n:]
            away[2, part(r, 1 - u), :] = straight.astype(jnp.bfloat16)
            go(give(r, 2, 1 - u))
            middle[part(r, u), :] = passing

    def mine(r):
        total[whole(r), :] = product(r, 0) + emb[whole(r), :].astype(jnp.float32)

    def relay(r):
        for u in (0, 1):
            give(r, 0, u).wait_recv()
            value = middle[part(r, u), :] + back[0, part(r, u), :].astype(jnp.float32)
            away[1, part(r, u), :] = value.astype(jnp.bfloat16)
            go(give(r, 1, u))

    def finish(r):
        for n in (2, 1):
            for u in (0, 1):
                give(r, n, u).wait_recv()
        value = total[whole(r), :]
        for n in (2, 1):
            value = value + back[n, whole(r), :].astype(jnp.float32)
        out[whole(r), :] = value.astype(jnp.bfloat16)

    greet(around(x, z))
    load = pltpu.make_async_copy(a, gathered.at[0], load_sem)
    load.start()
    load.wait()
    c = pl.ds(pl.multiple_of(x * quarter, quarter), quarter)
    weights = [pltpu.make_async_copy(wo_here.at[:, :, c], w.at[0], w_sem.at[0])] + [
        pltpu.make_async_copy(wo.at[:, k - 1], w.at[k], w_sem.at[k]) for k in range(1, RING)
    ]
    offer(0)
    offer(1)
    for copy in weights:
        copy.start()
    arrive(0)
    offer(2)
    for copy in weights:
        copy.wait()
    count = len(sizes)
    for r in range(count):
        far(r)
        if r + 1 < count:
            arrive(r + 1)
        if r + 3 < count:
            offer(r + 3)
        near(r)
        if r:
            relay(r - 1)
        mine(r)
        if r > 1:
            finish(r - 2)
    relay(count - 1)
    for r in (count - 2, count - 1):
        finish(r)
    for copy in started:
        copy.wait_send()


def output(a, w_out, wo, emb, sizes):
    rows, depth = a.shape
    cols = emb.shape[1]
    chunks = len(sizes)
    vmem = pl.BlockSpec(memory_space=pltpu.VMEM)
    hbm = pl.BlockSpec(memory_space=pl.ANY)
    dma = pltpu.SemaphoreType.DMA
    return pl.pallas_call(
        functools.partial(output_kernel, sizes=sizes),
        out_shape=jax.ShapeDtypeStruct((rows, cols), jnp.bfloat16),
        in_specs=[hbm, hbm, hbm, vmem],
        out_specs=vmem,
        scratch_shapes=[
            pltpu.VMEM((RING, rows, depth), jnp.bfloat16),
            pltpu.VMEM((RING,) + wo.shape[:1] + wo.shape[2:], jnp.bfloat16),
            pltpu.VMEM((3, rows, cols), jnp.bfloat16),
            pltpu.VMEM((3, rows, cols), jnp.bfloat16),
            pltpu.VMEM((rows, cols), jnp.float32),
            pltpu.VMEM((rows, cols), jnp.float32),
            dma,
            dma((RING,)),
            dma((chunks, 4)),
            dma((chunks, 4)),
            dma((chunks, 6)),
            dma((chunks, 6)),
        ],
        compiler_params=pltpu.CompilerParams(
            collective_id=1, has_side_effects=True, vmem_limit_bytes=48 * MIB
        ),
        cost_estimate=pl.CostEstimate(
            flops=2 * rows * depth * RING * RING * cols, bytes_accessed=150 * MIB, transcendentals=0
        ),
        name="output",
    )(a, w_out.reshape(wo.shape[0], wo.shape[2], w_out.shape[1]), wo, emb)


def body(embedded, norm_gain, w_query, w_keyval, w_out, prefix_kv, prefix_len, needed, row_slot):
    steps, rows, width = embedded.shape
    q, own, cache, wo, begin = project(
        embedded, w_query, w_keyval, norm_gain[None], row_slot, needed, prefix_len, prefix_kv, w_out
    )
    q = q.reshape(steps, rows, q.shape[1])
    own = own.reshape(steps, rows, own.shape[1])
    attended = attend(begin, needed, prefix_len, q, own, cache, prefix_kv.shape[0])
    mixed = output(
        attended.reshape(steps * rows, width),
        w_out,
        wo,
        embedded.reshape(steps * rows, width),
        (128,) * (steps * rows // 128),
    )
    return mixed.reshape(steps, rows, width)


def solution(mesh):
    in_specs = (
        P(None, "grp", "tp"),
        P(),
        P(None, "tp"),
        P(None, "tp"),
        P("tp", None),
        P("grp", None, "tp"),
        P(),
        P(),
        P("grp", None),
    )
    out_specs = P(None, "grp", "tp")
    return jax.shard_map(body, mesh=mesh, in_specs=in_specs, out_specs=out_specs, check_vma=False)
```

```python
import functools
import math

import jax
import jax.numpy as jnp
from jax import lax
from jax.experimental import pallas as pl
from jax.experimental.pallas import tpu as pltpu
from jax.sharding import PartitionSpec as P

HEAD = 128
HALF = 64
RING = 4
EPSILON = 1e-05
ROPE_THETA = 500000.0
SUB = 32
FIRST_ROWS = 544
MIB = 1 << 20
MESH = pl.DeviceIdType.MESH
ORDER = (0, 3, 1, 2)


def place():
    t = lax.axis_index("tp")
    return t, lax.div(t, RING), lax.rem(t, RING)


def index_of(x, z):
    return lax.rem(x, RING) * RING + lax.rem(z, RING)


def greet(partners):
    barrier = pltpu.get_barrier_semaphore()
    for device in partners:
        pl.semaphore_signal(barrier, inc=1, device_id=device, device_id_type=MESH)
    pl.semaphore_wait(barrier, len(partners))


def around(x, z):
    return [{"tp": index_of(x + a, z + b)} for a, b in ((1, 0), (3, 0), (0, 1), (0, 3))]


def project_kernel(
    emb, wq, wkv, gain, row_slot, needed, lengths, prefix, prefix_halves, wo_here,
    q_out, kv_out, cache, wo, begin,
    blocks_a, blocks_b, w_q, w_kv, acc, squares, cosine, sine, kv_other, mine, table,
    load_sem, w_sem, send_sem, recv_sem, kv_sem, side_send, side_recv,
):
    all_rows, width = emb.shape
    rows = all_rows // 2
    q_cols = wq.shape[1]
    t, x, z = place()
    blocks = (blocks_a, blocks_b)
    halves = tuple(ref.shape[1] // 2 for ref in blocks)
    firsts = (0, 2 * halves[0])

    def slot_of(s, along, across):
        return index_of(x + across, z + along) if s == 0 else index_of(x + along, z + across)

    def neighbour(s, phase, d):
        on_z = (s == 0) == (phase == 0)
        return {"tp": index_of(x, z + d) if on_z else index_of(x + d, z)}

    def move(s, phase, o, kind, slot, d):
        ref = blocks[s].at[slot]
        if kind == 2:
            ref = blocks[s].at[slot, pl.ds(0, halves[s])]
        if kind == 3:
            ref = blocks[s].at[slot, pl.ds(halves[s], halves[s])]
        i = o if phase else RING
        return pltpu.make_async_remote_copy(
            src_ref=ref,
            dst_ref=ref,
            send_sem=send_sem.at[s, i, kind],
            recv_sem=recv_sem.at[s, i, kind],
            device_id=neighbour(s, phase, d),
            device_id_type=MESH,
        )

    def at(s, phase, o, far):
        return slot_of(s, far, 0) if phase == 0 else slot_of(s, ORDER[o], far)

    started = []

    def start(*a):
        copy = move(*a)
        copy.start()
        started.append(copy)

    def send(s, phase, o):
        slot = at(s, phase, o, 0)
        start(s, phase, o, 0, slot, 1)
        start(s, phase, o, 1, slot, RING - 1)

    def pass_on(s, phase, o):
        back, ahead = at(s, phase, o, 3), at(s, phase, o, 1)
        move(s, phase, o, 0, back, 1).wait_recv()
        start(s, phase, o, 2, back, 1)
        move(s, phase, o, 1, ahead, 1).wait_recv()
        start(s, phase, o, 3, ahead, RING - 1)

    def opposite(s, phase, o):
        slot = at(s, phase, o, 2)
        move(s, phase, o, 2, slot, 1).wait_recv()
        move(s, phase, o, 3, slot, 1).wait_recv()

    def multiply(*todo):
        for s in (0, 1):
            slots = [slot for other, slot in todo if other == s]
            if slots:
                accumulate(s, slots)

    def accumulate(s, slots):
        half = halves[s]

        def one(i, _):
            which, lower = lax.div(i, 2), lax.rem(i, 2)
            slot = slots[0]
            for j in range(1, len(slots)):
                slot = jnp.where(which == j, slots[j], slot)
            value = blocks[s][slot, pl.ds(pl.multiple_of(lower * half, 16), half), :]
            value = value.astype(jnp.float32)
            r = pl.ds(pl.multiple_of(firsts[s] + lower * half, 16), half)
            square = value * value
            total = square[:, :128]
            for c in range(1, width // 128):
                total = total + square[:, c * 128 : (c + 1) * 128]
            squares[r, :] += total
            depth = pl.ds(pl.multiple_of(slot * width, width), width)
            scaled = (value * gain[:, depth]).astype(jnp.bfloat16)
            for ref, c in ((w_q, pl.ds(0, q_cols)), (w_kv, pl.ds(q_cols, HEAD))):
                acc[r, c] += jnp.dot(scaled, ref[depth, :], preferred_element_type=jnp.float32)
            return 0

        lax.fori_loop(0, 2 * len(slots), one, 0)

    g = lax.axis_index("grp")
    y, core = lax.div(g, 2), lax.rem(g, 2)
    upper = lax.rem(t, 2)
    n_short = prefix_halves.shape[0] // 2
    n_long = 2 * n_short
    piece = wo.shape[2]
    quarter = wo.shape[3]
    cut = piece // 2
    other_half = {"tp": t + 1 - 2 * upper}
    sibling = {"grp": g + 1 - 2 * core}

    def group(a, flip=False):
        return lax.rem(y + a, RING) * 2 + (1 - core if flip else core)

    def up(d):
        return {"grp": group(d)}

    def side(n, src, dst, device):
        return pltpu.make_async_remote_copy(
            src_ref=src,
            dst_ref=dst,
            send_sem=side_send.at[n],
            recv_sem=side_recv.at[n],
            device_id=device,
            device_id_type=MESH,
        )

    def go(copy):
        copy.start()
        started.append(copy)

    def pair():
        return side(0, mine, cache.at[1, g], other_half)

    def cache_ring(h, d, group_id):
        ref = cache.at[h, group_id]
        return side(1 + 2 * h + (0 if d == 1 else 1), ref if h else mine, ref, up(d))

    def cache_forward(h, group_id):
        ref = cache.at[h, group_id]
        return side(5 + h, ref, ref, up(1 if h == 0 else RING - 1))

    def cache_sibling(h, a, flip=False):
        ref = cache.at[h, group(a, flip)]
        return side(7 + 4 * h + a, ref if h or a else mine, ref, sibling)

    def wo_line(k):
        c = pl.ds(pl.multiple_of(lax.rem(x + k, RING) * quarter, quarter), quarter)
        return side(
            14 + k, wo_here.at[g, :, c], wo.at[g, k - 1], {"tp": index_of(x + k, z)}
        )

    def wo_ring(d, group_id):
        ref = wo.at[group_id]
        return side(18 if d == 1 else 19, ref, ref, up(d))

    def wo_forward(d, group_id):
        ref = wo.at[group_id, :, pl.ds(0 if d == 1 else cut, cut)]
        return side(20 if d == 1 else 21, ref, ref, up(d))

    def wo_sibling(a, flip=False):
        ref = wo.at[group(a, flip)]
        return side(22 + a, ref, ref, sibling)

    ahead, back = 1, RING - 1

    def side_begin():
        go(pair())
        for d in (ahead, back):
            go(cache_ring(0, d, g))
        for k in (1, 2, 3):
            go(wo_line(k))

    def side_line():
        for k in (1, 2, 3):
            wo_line(k).wait_recv()
        for d in (ahead, back):
            go(wo_ring(d, g))
        go(wo_sibling(0))

    def side_pair():
        pair().wait_recv()
        for d in (ahead, back):
            go(cache_ring(1, d, g))
        for h in (0, 1):
            go(cache_sibling(h, 0))

    def side_cache(h):
        cache_ring(h, ahead, group(back)).wait_recv()
        if h == 0:
            go(cache_forward(h, group(back)))
        cache_ring(h, back, group(ahead)).wait_recv()
        if h == 1:
            go(cache_forward(h, group(ahead)))
        go(cache_sibling(h, back))
        go(cache_sibling(h, ahead))

    def side_wo():
        wo_ring(ahead, group(back)).wait_recv()
        go(wo_forward(ahead, group(back)))
        wo_ring(back, group(ahead)).wait_recv()
        go(wo_forward(back, group(ahead)))
        go(wo_sibling(back))
        go(wo_sibling(ahead))

    def side_cache_far(h):
        cache_forward(h, group(2)).wait_recv()
        go(cache_sibling(h, 2))

    def side_wo_far():
        wo_forward(ahead, group(2)).wait_recv()
        wo_forward(back, group(2)).wait_recv()
        go(wo_sibling(2))

    def side_end():
        for a in range(RING):
            for h in (0, 1):
                cache_sibling(h, a, True).wait_recv()
            wo_sibling(a, True).wait_recv()

    loads = [
        pltpu.make_async_copy(
            emb.at[pl.ds(firsts[s], 2 * halves[s])], blocks[s].at[t], load_sem.at[s]
        )
        for s in (0, 1)
    ]
    own_cache = [
        pltpu.make_async_copy(
            prefix.at[pl.ds(0, n_long)], mine.at[pl.ds(0, n_long)], load_sem.at[2]
        ),
        pltpu.make_async_copy(
            prefix_halves.at[pl.ds(n_short, n_short), 0],
            mine.at[pl.ds(n_long, n_short)],
            load_sem.at[3],
        ),
    ]
    weights = [
        pltpu.make_async_copy(wq, w_q, w_sem.at[0]),
        pltpu.make_async_copy(wkv, w_kv, w_sem.at[1]),
    ]
    for copy in loads + own_cache:
        copy.start()
    greet(
        around(x, z)
        + [{"tp": index_of(x + 2, z)}, sibling, up(ahead), up(back)]
    )
    for copy in loads:
        copy.wait()
    for copy in own_cache:
        copy.wait()
    side_begin()
    for s in (0, 1):
        send(s, 0, 0)
    keep = pltpu.make_async_copy(mine, cache.at[0, g], load_sem.at[4])
    keep.start()
    for copy in weights:
        copy.start()
    for s in (0, 1):
        send(s, 1, 0)
    acc[...] = jnp.zeros_like(acc)
    squares[...] = jnp.zeros_like(squares)

    names = table.shape[1] // 2
    line = lax.broadcasted_iota(jnp.int32, (2 * names, HEAD), 0)
    lane = lax.broadcasted_iota(jnp.int32, (2 * names, HEAD), 1)
    position = jnp.zeros((2 * names, HEAD), jnp.int32)
    starts = []
    for n in range(names):
        length = lengths[needed[g, n]]
        position = jnp.where(line == n, length, position)
        position = jnp.where(line == names + n, length + 1, position)
        starts.append(jnp.sum(jnp.where(row_slot[...] < n, 1, 0)))
        begin[n] = starts[n]
    pair_index = lax.div(lane, 2).astype(jnp.float32)
    inverse = jnp.exp(pair_index * (-2.0 * math.log(ROPE_THETA) / HEAD))
    angle = position.astype(jnp.float32) * inverse
    table[0] = jnp.cos(angle)
    table[1] = jnp.sin(angle) * jnp.where(lax.rem(lane, 2) == 0, -1.0, 1.0)

    def spread(i, _):
        s = lax.div(i * 128, rows)
        row = lax.broadcasted_iota(jnp.int32, (128, HEAD), 0) + lax.rem(i * 128, rows)
        for k, ref in ((0, cosine), (1, sine)):
            out = jnp.zeros((128, HEAD), jnp.float32)
            for n in range(names):
                out = jnp.where(row >= starts[n], table[k, pl.ds(s * names + n, 1), :], out)
            ref[pl.ds(pl.multiple_of(i * 128, 128), 128), :] = out
        return 0

    lax.fori_loop(0, all_rows // 128, spread, 0)
    for copy in weights:
        copy.wait()
    both = (0, 1)
    multiply((0, t), (1, t))
    side_line()
    side_cache(0)
    for s in both:
        pass_on(s, 0, 0)
    for o in (1, 2):
        for s in both:
            send(s, 1, o)
    multiply(*[(s, at(s, 0, 0, d)) for d in (3, 1) for s in both])
    side_pair()
    for s in both:
        pass_on(s, 1, 0)
    multiply(*[(s, at(s, 1, 0, d)) for d in (3, 1) for s in both])
    for s in both:
        opposite(s, 0, 0)
        send(s, 1, 3)
    multiply(*[(s, at(s, 0, 0, 2)) for s in both])
    side_wo()
    for o in (1, 2, 3):
        for s in both:
            pass_on(s, 1, o)
        multiply(*[(s, at(s, 1, o, d)) for d in (3, 1) for s in both])
        if o == 1:
            side_cache(1)
        if o == 2:
            side_cache_far(0)
            side_wo_far()
        if o == 3:
            side_cache_far(1)
        for s in both:
            opposite(s, 1, o - 1)
        multiply(*[(s, at(s, 1, o - 1, 2)) for s in both])
    def turn(v, c, n):
        even = lax.rem(lax.broadcasted_iota(jnp.int32, v.shape, 1), 2) == 0
        other = jnp.where(even, pltpu.roll(v, HEAD - 1, 1), pltpu.roll(v, 1, 1))
        return v * c + other * n

    def scale_of(r):
        mean = jnp.sum(squares[r, :], axis=1, keepdims=True) / (RING * RING * width)
        return lax.rsqrt(mean + EPSILON)

    def tile(s, i):
        return pl.ds(pl.multiple_of(firsts[s] + i * halves[s], 16), halves[s])

    def own_kv(s):
        def one(i, _):
            r = tile(s, i)
            v = acc[r, pl.ds(q_cols, HEAD)] * scale_of(r)
            c, n = cosine[r, :], sine[r, :]
            low = lax.broadcasted_iota(jnp.int32, v.shape, 1) < HALF
            c = jnp.where(upper == 0, c, pltpu.roll(c, HALF, 1))
            n = jnp.where(upper == 0, n, pltpu.roll(n, HALF, 1))
            kv_out[r, pl.ds(0, HEAD)] = jnp.where(low, turn(v, c, n), v).astype(jnp.bfloat16)
            return 0

        lax.fori_loop(0, 2, one, 0)

    def swap(s):
        r = pl.ds(firsts[s], 2 * halves[s])
        return pltpu.make_async_remote_copy(
            src_ref=kv_out.at[r, pl.ds(0, HEAD)],
            dst_ref=kv_other.at[r],
            send_sem=kv_sem.at[0, s],
            recv_sem=kv_sem.at[1, s],
            device_id=other_half,
            device_id_type=MESH,
        )

    def queries(s):
        def one(i, _):
            r = tile(s, i)
            scale = scale_of(r)
            c, n = cosine[r, :], sine[r, :]
            low = lax.broadcasted_iota(jnp.int32, c.shape, 1) < HALF
            for h in range(q_cols // HEAD):
                v = turn(acc[r, pl.ds(h * HEAD, HEAD)] * scale, c, n)
                rolled = pltpu.roll(v, HALF, 1)
                first = jnp.where(low, jnp.where(upper == 0, v, rolled), 0.0)
                second = jnp.where(low, jnp.where(upper == 0, rolled, v), 0.0)
                q_out[r, pl.ds(2 * h * HEAD, HEAD)] = first.astype(jnp.bfloat16)
                q_out[r, pl.ds((2 * h + 1) * HEAD, HEAD)] = second.astype(jnp.bfloat16)
            return 0

        lax.fori_loop(0, 2, one, 0)

    for s in both:
        opposite(s, 1, 3)
        multiply((s, at(s, 1, 3, 2)))
        own_kv(s)
        swap(s).start()
        queries(s)
    for s in both:
        swap(s).wait()
    kv_out[:, pl.ds(HEAD, HEAD)] = kv_other[...]
    side_end()
    keep.wait()
    for copy in started:
        copy.wait_send()


def project(emb, wq, wkv, gain, row_slot, needed, lengths, prefix_kv, w_out):
    groups, names = needed.shape
    steps, rows, width = emb.shape
    all_rows = steps * rows
    q_cols = wq.shape[1]
    heads = q_cols // HEAD
    vmem = pl.BlockSpec(memory_space=pltpu.VMEM)
    hbm = pl.BlockSpec(memory_space=pl.ANY)
    smem = pl.BlockSpec(memory_space=pltpu.SMEM)
    tp = RING * RING
    owned, longest, kv_width = prefix_kv.shape
    short = longest // 2
    depth, out_cols = w_out.shape
    return pl.pallas_call(
        project_kernel,
        out_shape=(
            jax.ShapeDtypeStruct((all_rows, heads * 2 * HEAD), jnp.bfloat16),
            jax.ShapeDtypeStruct((all_rows, 2 * HEAD), jnp.bfloat16),
            jax.ShapeDtypeStruct((2, groups, owned * 3 // 2, short, kv_width), jnp.bfloat16),
            jax.ShapeDtypeStruct(
                (groups, RING - 1, depth // groups, out_cols // RING), jnp.bfloat16
            ),
            jax.ShapeDtypeStruct((names,), jnp.int32),
        ),
        in_specs=[hbm, hbm, hbm, vmem, vmem, smem, smem, hbm, hbm, hbm],
        out_specs=(vmem, vmem, hbm, hbm, smem),
        scratch_shapes=[
            pltpu.VMEM((tp, FIRST_ROWS, width), jnp.bfloat16),
            pltpu.VMEM((tp, all_rows - FIRST_ROWS, width), jnp.bfloat16),
            pltpu.VMEM((tp * width, q_cols), jnp.bfloat16),
            pltpu.VMEM((tp * width, HEAD), jnp.bfloat16),
            pltpu.VMEM((all_rows, q_cols + HEAD), jnp.float32),
            pltpu.VMEM((all_rows, HEAD), jnp.float32),
            pltpu.VMEM((all_rows, HEAD), jnp.float32),
            pltpu.VMEM((all_rows, HEAD), jnp.float32),
            pltpu.VMEM((all_rows, HEAD), jnp.bfloat16),
            pltpu.VMEM((owned * 3 // 2, short, kv_width), jnp.bfloat16),
            pltpu.VMEM((2, 2 * names, HEAD), jnp.float32),
            pltpu.SemaphoreType.DMA((5,)),
            pltpu.SemaphoreType.DMA((2,)),
            pltpu.SemaphoreType.DMA((2, RING + 1, 4)),
            pltpu.SemaphoreType.DMA((2, RING + 1, 4)),
            pltpu.SemaphoreType.DMA((2, 2)),
            pltpu.SemaphoreType.DMA((26,)),
            pltpu.SemaphoreType.DMA((26,)),
        ],
        compiler_params=pltpu.CompilerParams(
            collective_id=0, has_side_effects=True, vmem_limit_bytes=58 * MIB
        ),
        cost_estimate=pl.CostEstimate(
            flops=2 * steps * rows * tp * width * (q_cols + HEAD),
            bytes_accessed=300 * MIB,
            transcendentals=0,
        ),
        name="project",
    )(
        emb.reshape(all_rows, width), wq, wkv, gain, row_slot, needed, lengths,
        prefix_kv.reshape(2 * owned, short, kv_width),
        prefix_kv.reshape(owned, 2, short, kv_width),
        w_out.reshape(groups, depth // groups, out_cols),
    )


def attend_kernel(
    begin, needed, lengths, q_here, own_here, cache, out,
    q, own, kv, items, scores, weights, kv_sem, in_sem, owned,
):
    steps, rows = q.shape[0], q.shape[1]
    heads = q.shape[2] // (2 * HEAD)
    many = steps * heads * SUB
    slots, longest = kv.shape[0], kv.shape[1]
    short = longest // 2
    n_long = owned // 2
    g = lax.axis_index("grp")
    upper = lax.rem(lax.axis_index("tp"), 2)
    factor = math.log2(math.e) / math.sqrt(HEAD)
    nt = (((1,), (1,)), ((), ()))

    def length_of(slot):
        return lengths[needed[g, slot]]

    def fetch(slot, half, size):
        prefix = needed[g, slot]
        owner, local = lax.div(prefix, owned), lax.rem(prefix, owned)
        block = owner * (owned + n_long) + jnp.where(local < n_long, 2 * local, local + n_long)
        return pltpu.make_async_copy(
            cache.at[half, pl.ds(pl.multiple_of(block * short, short), size)],
            kv.at[slot, pl.ds(0, size), pl.ds(half * HEAD, HEAD)],
            kv_sem.at[slot, half],
        )

    def each(slot, do):
        for size in (short, longest):

            @pl.when((length_of(slot) > short) == (size == longest))
            def _():
                for half in (0, 1):
                    do(fetch(slot, half, size))

        return 0

    inputs = [
        pltpu.make_async_copy(q_here, q, in_sem.at[0]),
        pltpu.make_async_copy(own_here, own, in_sem.at[1]),
    ]
    for copy in inputs:
        copy.start()
    lax.fori_loop(0, slots, lambda n, _: each(n, lambda copy: copy.start()), 0)

    def plan(slot, counts):
        lo = begin[slot]
        hi = jnp.where(slot == slots - 1, rows, begin[jnp.minimum(slot + 1, slots - 1)])
        long = length_of(slot) > short

        def add(i, counts):
            n = jnp.where(long, counts[0], counts[1])
            items[jnp.where(long, 0, 1), n] = slot * rows + i
            return counts[0] + jnp.where(long, 1, 0), counts[1] + jnp.where(long, 0, 1)

        return lax.fori_loop(lax.div(lo, SUB), lax.div(hi + SUB - 1, SUB), add, counts)

    n_items = lax.fori_loop(0, slots, plan, (jnp.int32(0), jnp.int32(0)))
    for copy in inputs:
        copy.wait()
    lax.fori_loop(0, slots, lambda n, _: each(n, lambda copy: copy.wait()), 0)

    def run(kind, size):
        def scores_of(e, item):
            slot, i = lax.div(item, rows), lax.rem(item, rows)
            r = pl.ds(pl.multiple_of(i * SUB, SUB), SUB)
            query = jnp.concatenate(
                [
                    q[s, r, pl.ds(h * 2 * HEAD, 2 * HEAD)]
                    for s in range(steps)
                    for h in range(heads)
                ],
                axis=0,
            )
            for first in range(0, size, short):
                keys = kv[slot, pl.ds(first, short), :]
                scores[e, :, pl.ds(first, short)] = lax.dot_general(
                    query, keys, nt, preferred_element_type=jnp.float32
                )
            mine = [own[s, r, :].astype(jnp.float32) for s in range(steps)]
            alone = []
            for s in range(steps):
                for h in range(heads):
                    one = q[s, r, pl.ds(h * 2 * HEAD, 2 * HEAD)].astype(jnp.float32)
                    alone.append(
                        [jnp.sum(one * key, axis=1, keepdims=True) for key in mine[: s + 1]]
                    )
            return slot, r, i, mine, alone

        def weigh(e, slot, alone):
            key = lax.broadcasted_iota(jnp.int32, (1, short), 1) + (size - short)
            last = jnp.where(key < length_of(slot), 0.0, -jnp.inf)
            totals, singles = [], []
            for m in range(0, many, SUB):
                rows_here = pl.ds(m, SUB)
                tiles = []
                for first in range(0, size, HEAD):
                    tile = scores[e, rows_here, pl.ds(first, HEAD)]
                    if first >= size - short:
                        c = first - (size - short)
                        tile = tile + last[:, c : c + HEAD]
                    tiles.append(tile)
                top = jnp.max(functools.reduce(jnp.maximum, tiles), axis=1, keepdims=True)
                extra = alone[m // SUB]
                top = functools.reduce(jnp.maximum, [top] + extra)
                extra = [jnp.exp2((one - top) * factor) for one in extra]
                tiles = [jnp.exp2((tile - top) * factor) for tile in tiles]
                total = jnp.sum(functools.reduce(jnp.add, tiles), axis=1, keepdims=True)
                totals.append(functools.reduce(jnp.add, [total] + extra))
                singles.append([one.astype(jnp.bfloat16).astype(jnp.float32) for one in extra])
                for n, tile in enumerate(tiles):
                    weights[e, rows_here, pl.ds(n * HEAD, HEAD)] = tile.astype(jnp.bfloat16)
            return totals, singles

        def values_of(e, slot, mine, totals, singles):
            summed = jnp.dot(
                weights[e, :, pl.ds(0, size)],
                kv[slot, pl.ds(0, size), :],
                preferred_element_type=jnp.float32,
            )
            out_blocks = []
            for n, total in enumerate(totals):
                block = summed[n * SUB : (n + 1) * SUB]
                for one, value in zip(singles[n], mine):
                    block = block + one * value
                block = block / total
                here, there = block[:, :HEAD], block[:, HEAD:]
                low = lax.broadcasted_iota(jnp.int32, here.shape, 1) < HALF
                first = jnp.where(upper == 0, here, there)
                second = jnp.where(upper == 0, there, here)
                out_blocks.append(jnp.where(low, pltpu.roll(first, HALF, 1), second))
            return out_blocks

        def store(slot, r, i, result):
            lo = begin[slot]
            hi = jnp.where(slot == slots - 1, rows, begin[jnp.minimum(slot + 1, slots - 1)])
            at_row = lax.broadcasted_iota(jnp.int32, (SUB, HEAD), 0) + i * SUB
            inside = (at_row >= lo) & (at_row < hi)
            for s in range(steps):
                for h in range(heads):
                    c = pl.ds(h * HEAD, HEAD)
                    before = out[s, r, c].astype(jnp.float32)
                    out[s, r, c] = jnp.where(inside, result[s * heads + h], before).astype(
                        jnp.bfloat16
                    )

        def two(p, _):
            last = n_items[kind] - 1
            taken = [items[kind, jnp.minimum(2 * p + e, last)] for e in (0, 1)]
            scored = [scores_of(e, taken[e]) for e in (0, 1)]
            soft = [weigh(e, scored[e][0], scored[e][4]) for e in (0, 1)]
            results = [values_of(e, scored[e][0], scored[e][3], *soft[e]) for e in (0, 1)]
            for (slot, r, i, _, _), result in zip(scored, results):
                store(slot, r, i, result)
            return 0

        lax.fori_loop(0, lax.div(n_items[kind] + 1, 2), two, 0)

    run(0, longest)
    run(1, short)


def attend(begin, needed, lengths, q, own, cache, owned):
    steps, rows, wide = q.shape
    slots = needed.shape[1]
    short, kv_width = cache.shape[3:]
    cache = cache.reshape(2, -1, kv_width)
    vmem = pl.BlockSpec(memory_space=pltpu.VMEM)
    smem = pl.BlockSpec(memory_space=pltpu.SMEM)
    hbm = pl.BlockSpec(memory_space=pl.ANY)
    heads = wide // (2 * HEAD)
    return pl.pallas_call(
        functools.partial(attend_kernel, owned=owned),
        out_shape=jax.ShapeDtypeStruct((steps, rows, wide // 2), jnp.bfloat16),
        in_specs=[smem, smem, smem, hbm, hbm, hbm],
        out_specs=vmem,
        scratch_shapes=[
            pltpu.VMEM(q.shape, jnp.bfloat16),
            pltpu.VMEM(own.shape, jnp.bfloat16),
            pltpu.VMEM((slots, 2 * short, 2 * kv_width), jnp.bfloat16),
            pltpu.SMEM((2, rows // SUB + slots), jnp.int32),
            pltpu.VMEM((2, steps * heads * SUB, 2 * short), jnp.float32),
            pltpu.VMEM((2, steps * heads * SUB, 2 * short), jnp.bfloat16),
            pltpu.SemaphoreType.DMA((slots, 2)),
            pltpu.SemaphoreType.DMA((2,)),
        ],
        compiler_params=pltpu.CompilerParams(vmem_limit_bytes=54 * MIB),
        cost_estimate=pl.CostEstimate(
            flops=8 * 10**9, bytes_accessed=60 * MIB, transcendentals=5 * 10**6
        ),
        name="attend",
    )(begin, needed, lengths, q, own, cache)


def output_kernel(
    a, wo_here, wo, emb, out, gathered, w, away, back, middle, total,
    load_sem, w_sem, ag_send, ag_recv, rs_send, rs_recv, sizes,
):
    depth, cols = a.shape[1], out.shape[1]
    t, x, z = place()
    quarter = wo.shape[3]
    firsts = [sum(sizes[:r]) for r in range(len(sizes))]
    ahead, behind = 1, RING - 1
    ways = (ahead, behind)
    started = []

    def go(copy):
        copy.start()
        started.append(copy)

    def whole(r):
        return pl.ds(firsts[r], sizes[r])

    def part(r, u):
        return pl.ds(firsts[r] + u * (sizes[r] // 2), sizes[r] // 2)

    def line(d):
        return {"tp": index_of(x + d, z)}

    def column(d):
        return {"tp": index_of(x, z + d)}

    def remote(src, dst, sends, recvs, device):
        return pltpu.make_async_remote_copy(
            src_ref=src,
            dst_ref=dst,
            send_sem=sends,
            recv_sem=recvs,
            device_id=device,
            device_id_type=MESH,
        )

    def share(r, d):
        i = 0 if d == ahead else 1
        return remote(
            gathered.at[0, whole(r)], gathered.at[d, whole(r)],
            ag_send.at[r, i], ag_recv.at[r, i], line(d),
        )

    def forward(r, u):
        return remote(
            gathered.at[ways[u], part(r, u)], gathered.at[2, part(r, u)],
            ag_send.at[r, 2 + u], ag_recv.at[r, 2 + u], line(ways[u]),
        )

    def give(r, n, u):
        return remote(
            away.at[n, part(r, u)], back.at[n, part(r, u)],
            rs_send.at[r, 2 * n + u], rs_recv.at[r, 2 * n + u],
            column(ways[u] if n < 2 else ways[1 - u]),
        )

    def offer(r):
        for d in ways:
            go(share(r, d))

    def arrive(r):
        for u in (0, 1):
            share(r, ways[u]).wait_recv()
            go(forward(r, u))

    def product(r, d):
        c = pl.ds(pl.multiple_of(lax.rem(z + d, RING) * cols, cols), cols)
        result = None
        for k in range(RING):
            term = jnp.dot(
                gathered[k, whole(r), :],
                w[k, :, :, c].reshape(depth, cols),
                preferred_element_type=jnp.float32,
            )
            result = term if result is None else result + term
        return result

    def far(r):
        for u in (0, 1):
            forward(r, u).wait_recv()
        away[0, whole(r), :] = product(r, 2).astype(jnp.bfloat16)
        for u in (0, 1):
            go(give(r, 0, u))

    def near(r):
        n = sizes[r] // 2
        for u in (0, 1):
            value = product(r, ways[u])
            straight = value[n:] if u == 0 else value[:n]
            passing = value[:n] if u == 0 else value[n:]
            away[2, part(r, 1 - u), :] = straight.astype(jnp.bfloat16)
            go(give(r, 2, 1 - u))
            middle[part(r, u), :] = passing

    def mine(r):
        total[whole(r), :] = product(r, 0) + emb[whole(r), :].astype(jnp.float32)

    def relay(r):
        for u in (0, 1):
            give(r, 0, u).wait_recv()
            value = middle[part(r, u), :] + back[0, part(r, u), :].astype(jnp.float32)
            away[1, part(r, u), :] = value.astype(jnp.bfloat16)
            go(give(r, 1, u))

    def finish(r):
        for n in (2, 1):
            for u in (0, 1):
                give(r, n, u).wait_recv()
        value = total[whole(r), :]
        for n in (2, 1):
            value = value + back[n, whole(r), :].astype(jnp.float32)
        out[whole(r), :] = value.astype(jnp.bfloat16)

    load = pltpu.make_async_copy(a, gathered.at[0], load_sem)
    load.start()
    greet(around(x, z))
    load.wait()
    c = pl.ds(pl.multiple_of(x * quarter, quarter), quarter)
    weights = [pltpu.make_async_copy(wo_here.at[:, :, c], w.at[0], w_sem.at[0])] + [
        pltpu.make_async_copy(wo.at[:, k - 1], w.at[k], w_sem.at[k]) for k in range(1, RING)
    ]
    offer(0)
    offer(1)
    for copy in weights:
        copy.start()
    arrive(0)
    offer(2)
    for copy in weights:
        copy.wait()
    count = len(sizes)
    for r in range(count):
        far(r)
        if r + 1 < count:
            arrive(r + 1)
        if r + 3 < count:
            offer(r + 3)
        near(r)
        if r:
            relay(r - 1)
        mine(r)
        if r > 1:
            finish(r - 2)
    relay(count - 1)
    for r in (count - 2, count - 1):
        finish(r)
    for copy in started:
        copy.wait_send()


def output(a, w_out, wo, emb, sizes):
    rows, depth = a.shape
    cols = emb.shape[1]
    chunks = len(sizes)
    vmem = pl.BlockSpec(memory_space=pltpu.VMEM)
    hbm = pl.BlockSpec(memory_space=pl.ANY)
    dma = pltpu.SemaphoreType.DMA
    return pl.pallas_call(
        functools.partial(output_kernel, sizes=sizes),
        out_shape=jax.ShapeDtypeStruct((rows, cols), jnp.bfloat16),
        in_specs=[hbm, hbm, hbm, vmem],
        out_specs=vmem,
        scratch_shapes=[
            pltpu.VMEM((RING, rows, depth), jnp.bfloat16),
            pltpu.VMEM((RING,) + wo.shape[:1] + wo.shape[2:], jnp.bfloat16),
            pltpu.VMEM((3, rows, cols), jnp.bfloat16),
            pltpu.VMEM((3, rows, cols), jnp.bfloat16),
            pltpu.VMEM((rows, cols), jnp.float32),
            pltpu.VMEM((rows, cols), jnp.float32),
            dma,
            dma((RING,)),
            dma((chunks, 4)),
            dma((chunks, 4)),
            dma((chunks, 6)),
            dma((chunks, 6)),
        ],
        compiler_params=pltpu.CompilerParams(
            collective_id=1, has_side_effects=True, vmem_limit_bytes=48 * MIB
        ),
        cost_estimate=pl.CostEstimate(
            flops=2 * rows * depth * RING * RING * cols, bytes_accessed=150 * MIB, transcendentals=0
        ),
        name="output",
    )(a, w_out.reshape(wo.shape[0], wo.shape[2], w_out.shape[1]), wo, emb)


def body(embedded, norm_gain, w_query, w_keyval, w_out, prefix_kv, prefix_len, needed, row_slot):
    steps, rows, width = embedded.shape
    q, own, cache, wo, begin = project(
        embedded, w_query, w_keyval, norm_gain[None], row_slot, needed, prefix_len, prefix_kv, w_out
    )
    q = q.reshape(steps, rows, q.shape[1])
    own = own.reshape(steps, rows, own.shape[1])
    attended = attend(begin, needed, prefix_len, q, own, cache, prefix_kv.shape[0])
    mixed = output(
        attended.reshape(steps * rows, width),
        w_out,
        wo,
        embedded.reshape(steps * rows, width),
        (128,) * (steps * rows // 128),
    )
    return mixed.reshape(steps, rows, width)


def solution(mesh):
    in_specs = (
        P(None, "grp", "tp"),
        P(),
        P(None, "tp"),
        P(None, "tp"),
        P("tp", None),
        P("grp", None, "tp"),
        P(),
        P(),
        P("grp", None),
    )
    out_specs = P(None, "grp", "tp")
    return jax.shard_map(body, mesh=mesh, in_specs=in_specs, out_specs=out_specs, check_vma=False)
```

```python
import functools
import math

import jax
import jax.numpy as jnp
from jax import lax
from jax.experimental import pallas as pl
from jax.experimental.pallas import tpu as pltpu
from jax.sharding import PartitionSpec as P

HEAD = 128
HALF = 64
RING = 4
EPSILON = 1e-05
ROPE_THETA = 500000.0
SUB = 32
FIRST_ROWS = 544
MIB = 1 << 20
MESH = pl.DeviceIdType.MESH
ORDER = (0, 3, 1, 2)


def place():
    t = lax.axis_index("tp")
    return t, lax.div(t, RING), lax.rem(t, RING)


def index_of(x, z):
    return lax.rem(x, RING) * RING + lax.rem(z, RING)


def greet(partners):
    barrier = pltpu.get_barrier_semaphore()
    for device in partners:
        pl.semaphore_signal(barrier, inc=1, device_id=device, device_id_type=MESH)
    pl.semaphore_wait(barrier, len(partners))


def around(x, z):
    return [{"tp": index_of(x + a, z + b)} for a, b in ((1, 0), (3, 0), (0, 1), (0, 3))]


def project_kernel(
    emb, wq, wkv, gain, row_slot, needed, lengths, prefix, prefix_halves, wo_here,
    q_out, kv_out, cache, wo, begin,
    q_rows, blocks_a, blocks_b, w_q, w_kv, acc, squares, cosine, sine, kv_other, mine, table,
    load_sem, w_sem, send_sem, recv_sem, kv_sem, q_sem, side_send, side_recv,
):
    all_rows, width = emb.shape
    rows = all_rows // 2
    q_cols = wq.shape[1]
    t, x, z = place()
    blocks = (blocks_a, blocks_b)
    halves = tuple(ref.shape[1] // 2 for ref in blocks)
    firsts = (0, 2 * halves[0])

    def slot_of(s, along, across):
        return index_of(x + across, z + along) if s == 0 else index_of(x + along, z + across)

    def neighbour(s, phase, d):
        on_z = (s == 0) == (phase == 0)
        return {"tp": index_of(x, z + d) if on_z else index_of(x + d, z)}

    def move(s, phase, o, kind, slot, d):
        ref = blocks[s].at[slot]
        if kind == 2:
            ref = blocks[s].at[slot, pl.ds(0, halves[s])]
        if kind == 3:
            ref = blocks[s].at[slot, pl.ds(halves[s], halves[s])]
        i = o if phase else RING
        return pltpu.make_async_remote_copy(
            src_ref=ref,
            dst_ref=ref,
            send_sem=send_sem.at[s, i, kind],
            recv_sem=recv_sem.at[s, i, kind],
            device_id=neighbour(s, phase, d),
            device_id_type=MESH,
        )

    def at(s, phase, o, far):
        return slot_of(s, far, 0) if phase == 0 else slot_of(s, ORDER[o], far)

    started = []

    def start(*a):
        copy = move(*a)
        copy.start()
        started.append(copy)

    def send(s, phase, o):
        slot = at(s, phase, o, 0)
        start(s, phase, o, 0, slot, 1)
        start(s, phase, o, 1, slot, RING - 1)

    def pass_on(s, phase, o):
        back, ahead = at(s, phase, o, 3), at(s, phase, o, 1)
        move(s, phase, o, 0, back, 1).wait_recv()
        start(s, phase, o, 2, back, 1)
        move(s, phase, o, 1, ahead, 1).wait_recv()
        start(s, phase, o, 3, ahead, RING - 1)

    def opposite(s, phase, o):
        slot = at(s, phase, o, 2)
        move(s, phase, o, 2, slot, 1).wait_recv()
        move(s, phase, o, 3, slot, 1).wait_recv()

    def multiply(*todo):
        for s in (0, 1):
            slots = [slot for other, slot in todo if other == s]
            if slots:
                accumulate(s, slots)

    def accumulate(s, slots):
        half = halves[s]

        def one(i, _):
            which, lower = lax.div(i, 2), lax.rem(i, 2)
            slot = slots[0]
            for j in range(1, len(slots)):
                slot = jnp.where(which == j, slots[j], slot)
            value = blocks[s][slot, pl.ds(pl.multiple_of(lower * half, 16), half), :]
            value = value.astype(jnp.float32)
            r = pl.ds(pl.multiple_of(firsts[s] + lower * half, 16), half)
            square = value * value
            total = square[:, :128]
            for c in range(1, width // 128):
                total = total + square[:, c * 128 : (c + 1) * 128]
            squares[r, :] += total
            depth = pl.ds(pl.multiple_of(slot * width, width), width)
            scaled = (value * gain[:, depth]).astype(jnp.bfloat16)
            for ref, c in ((w_q, pl.ds(0, q_cols)), (w_kv, pl.ds(q_cols, HEAD))):
                acc[r, c] += jnp.dot(scaled, ref[depth, :], preferred_element_type=jnp.float32)
            return 0

        lax.fori_loop(0, 2 * len(slots), one, 0)

    g = lax.axis_index("grp")
    y, core = lax.div(g, 2), lax.rem(g, 2)
    upper = lax.rem(t, 2)
    n_short = prefix_halves.shape[0] // 2
    n_long = 2 * n_short
    piece = wo.shape[2]
    quarter = wo.shape[3]
    cut = piece // 2
    other_half = {"tp": t + 1 - 2 * upper}
    sibling = {"grp": g + 1 - 2 * core}

    def group(a, flip=False):
        return lax.rem(y + a, RING) * 2 + (1 - core if flip else core)

    def up(d):
        return {"grp": group(d)}

    def side(n, src, dst, device):
        return pltpu.make_async_remote_copy(
            src_ref=src,
            dst_ref=dst,
            send_sem=side_send.at[n],
            recv_sem=side_recv.at[n],
            device_id=device,
            device_id_type=MESH,
        )

    def go(copy):
        copy.start()
        started.append(copy)

    def pair():
        return side(0, mine, cache.at[1, g], other_half)

    def cache_ring(h, d, group_id):
        ref = cache.at[h, group_id]
        return side(1 + 2 * h + (0 if d == 1 else 1), ref if h else mine, ref, up(d))

    def cache_forward(h, group_id):
        ref = cache.at[h, group_id]
        return side(5 + h, ref, ref, up(1 if h == 0 else RING - 1))

    def cache_sibling(h, a, flip=False):
        ref = cache.at[h, group(a, flip)]
        return side(7 + 4 * h + a, ref if h or a else mine, ref, sibling)

    def wo_line(k):
        c = pl.ds(pl.multiple_of(lax.rem(x + k, RING) * quarter, quarter), quarter)
        return side(
            14 + k, wo_here.at[g, :, c], wo.at[g, k - 1], {"tp": index_of(x + k, z)}
        )

    def wo_ring(d, group_id):
        ref = wo.at[group_id]
        return side(18 if d == 1 else 19, ref, ref, up(d))

    def wo_forward(d, group_id):
        ref = wo.at[group_id, :, pl.ds(0 if d == 1 else cut, cut)]
        return side(20 if d == 1 else 21, ref, ref, up(d))

    def wo_sibling(a, flip=False):
        ref = wo.at[group(a, flip)]
        return side(22 + a, ref, ref, sibling)

    ahead, back = 1, RING - 1

    def side_begin():
        go(pair())
        for d in (ahead, back):
            go(cache_ring(0, d, g))
        for k in (1, 2, 3):
            go(wo_line(k))

    def side_line():
        for k in (1, 2, 3):
            wo_line(k).wait_recv()
        for d in (ahead, back):
            go(wo_ring(d, g))
        go(wo_sibling(0))

    def side_pair():
        pair().wait_recv()
        for d in (ahead, back):
            go(cache_ring(1, d, g))
        for h in (0, 1):
            go(cache_sibling(h, 0))

    def side_cache(h):
        cache_ring(h, ahead, group(back)).wait_recv()
        if h == 0:
            go(cache_forward(h, group(back)))
        cache_ring(h, back, group(ahead)).wait_recv()
        if h == 1:
            go(cache_forward(h, group(ahead)))
        go(cache_sibling(h, back))
        go(cache_sibling(h, ahead))

    def side_wo():
        wo_ring(ahead, group(back)).wait_recv()
        go(wo_forward(ahead, group(back)))
        wo_ring(back, group(ahead)).wait_recv()
        go(wo_forward(back, group(ahead)))
        go(wo_sibling(back))
        go(wo_sibling(ahead))

    def side_cache_far(h):
        cache_forward(h, group(2)).wait_recv()
        go(cache_sibling(h, 2))

    def side_wo_far():
        wo_forward(ahead, group(2)).wait_recv()
        wo_forward(back, group(2)).wait_recv()
        go(wo_sibling(2))

    def side_end():
        for a in range(RING):
            for h in (0, 1):
                cache_sibling(h, a, True).wait_recv()
            wo_sibling(a, True).wait_recv()

    loads = [
        pltpu.make_async_copy(
            emb.at[pl.ds(firsts[s], 2 * halves[s])], blocks[s].at[t], load_sem.at[s]
        )
        for s in (0, 1)
    ]
    own_cache = [
        pltpu.make_async_copy(
            prefix.at[pl.ds(0, n_long)], mine.at[pl.ds(0, n_long)], load_sem.at[2]
        ),
        pltpu.make_async_copy(
            prefix_halves.at[pl.ds(n_short, n_short), 0],
            mine.at[pl.ds(n_long, n_short)],
            load_sem.at[3],
        ),
    ]
    weights = [
        pltpu.make_async_copy(wq, w_q, w_sem.at[0]),
        pltpu.make_async_copy(wkv, w_kv, w_sem.at[1]),
    ]
    for copy in loads + own_cache:
        copy.start()
    greet(
        around(x, z)
        + [{"tp": index_of(x + 2, z)}, sibling, up(ahead), up(back)]
    )
    for copy in loads:
        copy.wait()
    for copy in own_cache:
        copy.wait()
    side_begin()
    for s in (0, 1):
        send(s, 0, 0)
    keep = pltpu.make_async_copy(mine, cache.at[0, g], load_sem.at[4])
    keep.start()
    for copy in weights:
        copy.start()
    for s in (0, 1):
        send(s, 1, 0)
    acc[...] = jnp.zeros_like(acc)
    squares[...] = jnp.zeros_like(squares)

    names = table.shape[1] // 2
    line = lax.broadcasted_iota(jnp.int32, (2 * names, HEAD), 0)
    lane = lax.broadcasted_iota(jnp.int32, (2 * names, HEAD), 1)
    position = jnp.zeros((2 * names, HEAD), jnp.int32)
    starts = []
    for n in range(names):
        length = lengths[needed[g, n]]
        position = jnp.where(line == n, length, position)
        position = jnp.where(line == names + n, length + 1, position)
        starts.append(jnp.sum(jnp.where(row_slot[...] < n, 1, 0)))
        begin[n] = starts[n]
    pair_index = lax.div(lane, 2).astype(jnp.float32)
    inverse = jnp.exp(pair_index * (-2.0 * math.log(ROPE_THETA) / HEAD))
    angle = position.astype(jnp.float32) * inverse
    table[0] = jnp.cos(angle)
    table[1] = jnp.sin(angle) * jnp.where(lax.rem(lane, 2) == 0, -1.0, 1.0)

    def spread(i, _):
        s = lax.div(i * 128, rows)
        row = lax.broadcasted_iota(jnp.int32, (128, HEAD), 0) + lax.rem(i * 128, rows)
        for k, ref in ((0, cosine), (1, sine)):
            out = jnp.zeros((128, HEAD), jnp.float32)
            for n in range(names):
                out = jnp.where(row >= starts[n], table[k, pl.ds(s * names + n, 1), :], out)
            ref[pl.ds(pl.multiple_of(i * 128, 128), 128), :] = out
        return 0

    lax.fori_loop(0, all_rows // 128, spread, 0)
    for copy in weights:
        copy.wait()
    both = (0, 1)
    multiply((0, t), (1, t))
    side_line()
    side_cache(0)
    for s in both:
        pass_on(s, 0, 0)
    for o in (1, 2):
        for s in both:
            send(s, 1, o)
    multiply(*[(s, at(s, 0, 0, d)) for d in (3, 1) for s in both])
    side_pair()
    for s in both:
        pass_on(s, 1, 0)
    multiply(*[(s, at(s, 1, 0, d)) for d in (3, 1) for s in both])
    for s in both:
        opposite(s, 0, 0)
        send(s, 1, 3)
    multiply(*[(s, at(s, 0, 0, 2)) for s in both])
    side_wo()
    for o in (1, 2, 3):
        for s in both:
            pass_on(s, 1, o)
        multiply(*[(s, at(s, 1, o, d)) for d in (3, 1) for s in both])
        if o == 1:
            side_cache(1)
        if o == 2:
            side_cache_far(0)
            side_wo_far()
        if o == 3:
            side_cache_far(1)
        for s in both:
            opposite(s, 1, o - 1)
        multiply(*[(s, at(s, 1, o - 1, 2)) for s in both])
    def turn(v, c, n):
        even = lax.rem(lax.broadcasted_iota(jnp.int32, v.shape, 1), 2) == 0
        other = jnp.where(even, pltpu.roll(v, HEAD - 1, 1), pltpu.roll(v, 1, 1))
        return v * c + other * n

    def scale_of(r):
        mean = jnp.sum(squares[r, :], axis=1, keepdims=True) / (RING * RING * width)
        return lax.rsqrt(mean + EPSILON)

    def tile(s, i):
        return pl.ds(pl.multiple_of(firsts[s] + i * halves[s], 16), halves[s])

    def own_kv(s):
        def one(i, _):
            r = tile(s, i)
            v = acc[r, pl.ds(q_cols, HEAD)] * scale_of(r)
            c, n = cosine[r, :], sine[r, :]
            low = lax.broadcasted_iota(jnp.int32, v.shape, 1) < HALF
            c = jnp.where(upper == 0, c, pltpu.roll(c, HALF, 1))
            n = jnp.where(upper == 0, n, pltpu.roll(n, HALF, 1))
            kv_out[r, pl.ds(0, HEAD)] = jnp.where(low, turn(v, c, n), v).astype(jnp.bfloat16)
            return 0

        lax.fori_loop(0, 2, one, 0)

    def swap(s):
        r = pl.ds(firsts[s], 2 * halves[s])
        return pltpu.make_async_remote_copy(
            src_ref=kv_out.at[r, pl.ds(0, HEAD)],
            dst_ref=kv_other.at[r],
            send_sem=kv_sem.at[0, s],
            recv_sem=kv_sem.at[1, s],
            device_id=other_half,
            device_id_type=MESH,
        )

    def queries(s):
        def one(i, _):
            r = tile(s, i)
            scale = scale_of(r)
            c, n = cosine[r, :], sine[r, :]
            low = lax.broadcasted_iota(jnp.int32, c.shape, 1) < HALF
            for h in range(q_cols // HEAD):
                v = turn(acc[r, pl.ds(h * HEAD, HEAD)] * scale, c, n)
                rolled = pltpu.roll(v, HALF, 1)
                first = jnp.where(low, jnp.where(upper == 0, v, rolled), 0.0)
                second = jnp.where(low, jnp.where(upper == 0, rolled, v), 0.0)
                q_rows[r, pl.ds(2 * h * HEAD, HEAD)] = first.astype(jnp.bfloat16)
                q_rows[r, pl.ds((2 * h + 1) * HEAD, HEAD)] = second.astype(jnp.bfloat16)
            return 0

        lax.fori_loop(0, 2, one, 0)

    def write(s):
        r = pl.ds(firsts[s], 2 * halves[s])
        return pltpu.make_async_copy(q_rows.at[r], q_out.at[r], q_sem.at[s])

    for s in both:
        opposite(s, 1, 3)
        multiply((s, at(s, 1, 3, 2)))
        own_kv(s)
        swap(s).start()
        queries(s)
        write(s).start()
    for s in both:
        swap(s).wait()
    kv_out[:, pl.ds(HEAD, HEAD)] = kv_other[...]
    side_end()
    keep.wait()
    for s in both:
        write(s).wait()
    for copy in started:
        copy.wait_send()


def project(emb, wq, wkv, gain, row_slot, needed, lengths, prefix_kv, w_out):
    groups, names = needed.shape
    steps, rows, width = emb.shape
    all_rows = steps * rows
    q_cols = wq.shape[1]
    heads = q_cols // HEAD
    vmem = pl.BlockSpec(memory_space=pltpu.VMEM)
    hbm = pl.BlockSpec(memory_space=pl.ANY)
    smem = pl.BlockSpec(memory_space=pltpu.SMEM)
    tp = RING * RING
    owned, longest, kv_width = prefix_kv.shape
    short = longest // 2
    depth, out_cols = w_out.shape
    return pl.pallas_call(
        project_kernel,
        out_shape=(
            jax.ShapeDtypeStruct((all_rows, heads * 2 * HEAD), jnp.bfloat16),
            jax.ShapeDtypeStruct((all_rows, 2 * HEAD), jnp.bfloat16),
            jax.ShapeDtypeStruct((2, groups, owned * 3 // 2, short, kv_width), jnp.bfloat16),
            jax.ShapeDtypeStruct(
                (groups, RING - 1, depth // groups, out_cols // RING), jnp.bfloat16
            ),
            jax.ShapeDtypeStruct((names,), jnp.int32),
        ),
        in_specs=[hbm, hbm, hbm, vmem, vmem, smem, smem, hbm, hbm, hbm],
        out_specs=(hbm, vmem, hbm, hbm, smem),
        scratch_shapes=[
            pltpu.VMEM((all_rows, heads * 2 * HEAD), jnp.bfloat16),
            pltpu.VMEM((tp, FIRST_ROWS, width), jnp.bfloat16),
            pltpu.VMEM((tp, all_rows - FIRST_ROWS, width), jnp.bfloat16),
            pltpu.VMEM((tp * width, q_cols), jnp.bfloat16),
            pltpu.VMEM((tp * width, HEAD), jnp.bfloat16),
            pltpu.VMEM((all_rows, q_cols + HEAD), jnp.float32),
            pltpu.VMEM((all_rows, HEAD), jnp.float32),
            pltpu.VMEM((all_rows, HEAD), jnp.float32),
            pltpu.VMEM((all_rows, HEAD), jnp.float32),
            pltpu.VMEM((all_rows, HEAD), jnp.bfloat16),
            pltpu.VMEM((owned * 3 // 2, short, kv_width), jnp.bfloat16),
            pltpu.VMEM((2, 2 * names, HEAD), jnp.float32),
            pltpu.SemaphoreType.DMA((5,)),
            pltpu.SemaphoreType.DMA((2,)),
            pltpu.SemaphoreType.DMA((2, RING + 1, 4)),
            pltpu.SemaphoreType.DMA((2, RING + 1, 4)),
            pltpu.SemaphoreType.DMA((2, 2)),
            pltpu.SemaphoreType.DMA((2,)),
            pltpu.SemaphoreType.DMA((26,)),
            pltpu.SemaphoreType.DMA((26,)),
        ],
        compiler_params=pltpu.CompilerParams(
            collective_id=0, has_side_effects=True, vmem_limit_bytes=58 * MIB
        ),
        cost_estimate=pl.CostEstimate(
            flops=2 * steps * rows * tp * width * (q_cols + HEAD),
            bytes_accessed=300 * MIB,
            transcendentals=0,
        ),
        name="project",
    )(
        emb.reshape(all_rows, width), wq, wkv, gain, row_slot, needed, lengths,
        prefix_kv.reshape(2 * owned, short, kv_width),
        prefix_kv.reshape(owned, 2, short, kv_width),
        w_out.reshape(groups, depth // groups, out_cols),
    )


def attend_kernel(
    begin, needed, lengths, q_here, own_here, cache, out,
    q, own, kv, items, scores, weights, kv_sem, in_sem, owned,
):
    steps, rows = q.shape[0], q.shape[1]
    heads = q.shape[2] // (2 * HEAD)
    many = steps * heads * SUB
    slots, longest = kv.shape[0], kv.shape[1]
    short = longest // 2
    n_long = owned // 2
    g = lax.axis_index("grp")
    upper = lax.rem(lax.axis_index("tp"), 2)
    factor = math.log2(math.e) / math.sqrt(HEAD)
    nt = (((1,), (1,)), ((), ()))

    def length_of(slot):
        return lengths[needed[g, slot]]

    def fetch(slot, half, size):
        prefix = needed[g, slot]
        owner, local = lax.div(prefix, owned), lax.rem(prefix, owned)
        block = owner * (owned + n_long) + jnp.where(local < n_long, 2 * local, local + n_long)
        return pltpu.make_async_copy(
            cache.at[half, pl.ds(pl.multiple_of(block * short, short), size)],
            kv.at[slot, pl.ds(0, size), pl.ds(half * HEAD, HEAD)],
            kv_sem.at[slot, half],
        )

    def each(slot, do):
        for size in (short, longest):

            @pl.when((length_of(slot) > short) == (size == longest))
            def _():
                for half in (0, 1):
                    do(fetch(slot, half, size))

        return 0

    inputs = [
        pltpu.make_async_copy(q_here, q, in_sem.at[0]),
        pltpu.make_async_copy(own_here, own, in_sem.at[1]),
    ]
    for copy in inputs:
        copy.start()
    lax.fori_loop(0, slots, lambda n, _: each(n, lambda copy: copy.start()), 0)

    def plan(slot, counts):
        lo = begin[slot]
        hi = jnp.where(slot == slots - 1, rows, begin[jnp.minimum(slot + 1, slots - 1)])
        long = length_of(slot) > short

        def add(i, counts):
            n = jnp.where(long, counts[0], counts[1])
            items[jnp.where(long, 0, 1), n] = slot * rows + i
            return counts[0] + jnp.where(long, 1, 0), counts[1] + jnp.where(long, 0, 1)

        return lax.fori_loop(lax.div(lo, SUB), lax.div(hi + SUB - 1, SUB), add, counts)

    n_items = lax.fori_loop(0, slots, plan, (jnp.int32(0), jnp.int32(0)))
    for copy in inputs:
        copy.wait()

    def run(kind, size):
        def scores_of(e, item):
            slot, i = lax.div(item, rows), lax.rem(item, rows)
            r = pl.ds(pl.multiple_of(i * SUB, SUB), SUB)
            query = jnp.concatenate(
                [
                    q[s, r, pl.ds(h * 2 * HEAD, 2 * HEAD)]
                    for s in range(steps)
                    for h in range(heads)
                ],
                axis=0,
            )
            for first in range(0, size, short):
                keys = kv[slot, pl.ds(first, short), :]
                scores[e, :, pl.ds(first, short)] = lax.dot_general(
                    query, keys, nt, preferred_element_type=jnp.float32
                )
            mine = [own[s, r, :].astype(jnp.float32) for s in range(steps)]
            alone = []
            for s in range(steps):
                for h in range(heads):
                    one = q[s, r, pl.ds(h * 2 * HEAD, 2 * HEAD)].astype(jnp.float32)
                    alone.append(
                        [jnp.sum(one * key, axis=1, keepdims=True) for key in mine[: s + 1]]
                    )
            return slot, r, i, mine, alone

        def weigh(e, slot, alone):
            key = lax.broadcasted_iota(jnp.int32, (1, short), 1) + (size - short)
            last = jnp.where(key < length_of(slot), 0.0, -jnp.inf)
            totals, singles = [], []
            for m in range(0, many, SUB):
                rows_here = pl.ds(m, SUB)
                tiles = []
                for first in range(0, size, HEAD):
                    tile = scores[e, rows_here, pl.ds(first, HEAD)]
                    if first >= size - short:
                        c = first - (size - short)
                        tile = tile + last[:, c : c + HEAD]
                    tiles.append(tile)
                top = jnp.max(functools.reduce(jnp.maximum, tiles), axis=1, keepdims=True)
                extra = alone[m // SUB]
                top = functools.reduce(jnp.maximum, [top] + extra)
                extra = [jnp.exp2((one - top) * factor) for one in extra]
                tiles = [jnp.exp2((tile - top) * factor) for tile in tiles]
                total = jnp.sum(functools.reduce(jnp.add, tiles), axis=1, keepdims=True)
                totals.append(functools.reduce(jnp.add, [total] + extra))
                singles.append([one.astype(jnp.bfloat16).astype(jnp.float32) for one in extra])
                for n, tile in enumerate(tiles):
                    weights[e, rows_here, pl.ds(n * HEAD, HEAD)] = tile.astype(jnp.bfloat16)
            return totals, singles

        def values_of(e, slot, mine, totals, singles):
            summed = jnp.dot(
                weights[e, :, pl.ds(0, size)],
                kv[slot, pl.ds(0, size), :],
                preferred_element_type=jnp.float32,
            )
            out_blocks = []
            for n, total in enumerate(totals):
                block = summed[n * SUB : (n + 1) * SUB]
                for one, value in zip(singles[n], mine):
                    block = block + one * value
                block = block / total
                here, there = block[:, :HEAD], block[:, HEAD:]
                low = lax.broadcasted_iota(jnp.int32, here.shape, 1) < HALF
                first = jnp.where(upper == 0, here, there)
                second = jnp.where(upper == 0, there, here)
                out_blocks.append(jnp.where(low, pltpu.roll(first, HALF, 1), second))
            return out_blocks

        def store(slot, r, i, result):
            lo = begin[slot]
            hi = jnp.where(slot == slots - 1, rows, begin[jnp.minimum(slot + 1, slots - 1)])
            at_row = lax.broadcasted_iota(jnp.int32, (SUB, HEAD), 0) + i * SUB
            inside = (at_row >= lo) & (at_row < hi)
            for s in range(steps):
                for h in range(heads):
                    c = pl.ds(h * HEAD, HEAD)
                    before = out[s, r, c].astype(jnp.float32)
                    out[s, r, c] = jnp.where(inside, result[s * heads + h], before).astype(
                        jnp.bfloat16
                    )

        def two(p, _):
            last = n_items[kind] - 1
            taken = [items[kind, jnp.minimum(2 * p + e, last)] for e in (0, 1)]
            scored = [scores_of(e, taken[e]) for e in (0, 1)]
            soft = [weigh(e, scored[e][0], scored[e][4]) for e in (0, 1)]
            results = [values_of(e, scored[e][0], scored[e][3], *soft[e]) for e in (0, 1)]
            for (slot, r, i, _, _), result in zip(scored, results):
                store(slot, r, i, result)
            return 0

        lax.fori_loop(0, lax.div(n_items[kind] + 1, 2), two, 0)

    def arrived(size):
        def one(slot, _):
            @pl.when((length_of(slot) > short) == (size == longest))
            def _():
                for half in (0, 1):
                    fetch(slot, half, size).wait()

            return 0

        lax.fori_loop(0, slots, one, 0)

    arrived(longest)
    run(0, longest)
    arrived(short)
    run(1, short)


def attend(begin, needed, lengths, q, own, cache, owned):
    steps, rows, wide = q.shape
    slots = needed.shape[1]
    short, kv_width = cache.shape[3:]
    cache = cache.reshape(2, -1, kv_width)
    vmem = pl.BlockSpec(memory_space=pltpu.VMEM)
    smem = pl.BlockSpec(memory_space=pltpu.SMEM)
    hbm = pl.BlockSpec(memory_space=pl.ANY)
    heads = wide // (2 * HEAD)
    return pl.pallas_call(
        functools.partial(attend_kernel, owned=owned),
        out_shape=jax.ShapeDtypeStruct((steps, rows, wide // 2), jnp.bfloat16),
        in_specs=[smem, smem, smem, hbm, hbm, hbm],
        out_specs=vmem,
        scratch_shapes=[
            pltpu.VMEM(q.shape, jnp.bfloat16),
            pltpu.VMEM(own.shape, jnp.bfloat16),
            pltpu.VMEM((slots, 2 * short, 2 * kv_width), jnp.bfloat16),
            pltpu.SMEM((2, rows // SUB + slots), jnp.int32),
            pltpu.VMEM((2, steps * heads * SUB, 2 * short), jnp.float32),
            pltpu.VMEM((2, steps * heads * SUB, 2 * short), jnp.bfloat16),
            pltpu.SemaphoreType.DMA((slots, 2)),
            pltpu.SemaphoreType.DMA((2,)),
        ],
        compiler_params=pltpu.CompilerParams(vmem_limit_bytes=54 * MIB),
        cost_estimate=pl.CostEstimate(
            flops=8 * 10**9, bytes_accessed=60 * MIB, transcendentals=5 * 10**6
        ),
        name="attend",
    )(begin, needed, lengths, q, own, cache)


def output_kernel(
    a, wo_here, wo, emb, out, gathered, w, away, back, middle, total,
    load_sem, w_sem, ag_send, ag_recv, rs_send, rs_recv, sizes,
):
    depth, cols = a.shape[1], out.shape[1]
    t, x, z = place()
    quarter = wo.shape[3]
    firsts = [sum(sizes[:r]) for r in range(len(sizes))]
    ahead, behind = 1, RING - 1
    ways = (ahead, behind)
    started = []

    def go(copy):
        copy.start()
        started.append(copy)

    def whole(r):
        return pl.ds(firsts[r], sizes[r])

    def part(r, u):
        return pl.ds(firsts[r] + u * (sizes[r] // 2), sizes[r] // 2)

    def line(d):
        return {"tp": index_of(x + d, z)}

    def column(d):
        return {"tp": index_of(x, z + d)}

    def remote(src, dst, sends, recvs, device):
        return pltpu.make_async_remote_copy(
            src_ref=src,
            dst_ref=dst,
            send_sem=sends,
            recv_sem=recvs,
            device_id=device,
            device_id_type=MESH,
        )

    def share(r, d):
        i = 0 if d == ahead else 1
        return remote(
            gathered.at[0, whole(r)], gathered.at[d, whole(r)],
            ag_send.at[r, i], ag_recv.at[r, i], line(d),
        )

    def forward(r, u):
        return remote(
            gathered.at[ways[u], part(r, u)], gathered.at[2, part(r, u)],
            ag_send.at[r, 2 + u], ag_recv.at[r, 2 + u], line(ways[u]),
        )

    def give(r, n, u):
        return remote(
            away.at[n, part(r, u)], back.at[n, part(r, u)],
            rs_send.at[r, 2 * n + u], rs_recv.at[r, 2 * n + u],
            column(ways[u] if n < 2 else ways[1 - u]),
        )

    def offer(r):
        for d in ways:
            go(share(r, d))

    def arrive(r):
        for u in (0, 1):
            share(r, ways[u]).wait_recv()
            go(forward(r, u))

    def product(r, d):
        c = pl.ds(pl.multiple_of(lax.rem(z + d, RING) * cols, cols), cols)
        result = None
        for k in range(RING):
            term = jnp.dot(
                gathered[k, whole(r), :],
                w[k, :, :, c].reshape(depth, cols),
                preferred_element_type=jnp.float32,
            )
            result = term if result is None else result + term
        return result

    def far(r):
        for u in (0, 1):
            forward(r, u).wait_recv()
        away[0, whole(r), :] = product(r, 2).astype(jnp.bfloat16)
        for u in (0, 1):
            go(give(r, 0, u))

    def near(r):
        n = sizes[r] // 2
        for u in (0, 1):
            value = product(r, ways[u])
            straight = value[n:] if u == 0 else value[:n]
            passing = value[:n] if u == 0 else value[n:]
            away[2, part(r, 1 - u), :] = straight.astype(jnp.bfloat16)
            go(give(r, 2, 1 - u))
            middle[part(r, u), :] = passing

    def mine(r):
        total[whole(r), :] = product(r, 0) + emb[whole(r), :].astype(jnp.float32)

    def relay(r):
        for u in (0, 1):
            give(r, 0, u).wait_recv()
            value = middle[part(r, u), :] + back[0, part(r, u), :].astype(jnp.float32)
            away[1, part(r, u), :] = value.astype(jnp.bfloat16)
            go(give(r, 1, u))

    def finish(r):
        for n in (2, 1):
            for u in (0, 1):
                give(r, n, u).wait_recv()
        value = total[whole(r), :]
        for n in (2, 1):
            value = value + back[n, whole(r), :].astype(jnp.float32)
        out[whole(r), :] = value.astype(jnp.bfloat16)

    load = pltpu.make_async_copy(a, gathered.at[0], load_sem)
    load.start()
    greet(around(x, z))
    load.wait()
    c = pl.ds(pl.multiple_of(x * quarter, quarter), quarter)
    weights = [pltpu.make_async_copy(wo_here.at[:, :, c], w.at[0], w_sem.at[0])] + [
        pltpu.make_async_copy(wo.at[:, k - 1], w.at[k], w_sem.at[k]) for k in range(1, RING)
    ]
    offer(0)
    offer(1)
    for copy in weights:
        copy.start()
    arrive(0)
    offer(2)
    for copy in weights:
        copy.wait()
    count = len(sizes)
    for r in range(count):
        far(r)
        if r + 1 < count:
            arrive(r + 1)
        if r + 3 < count:
            offer(r + 3)
        near(r)
        if r:
            relay(r - 1)
        mine(r)
        if r > 1:
            finish(r - 2)
    relay(count - 1)
    for r in (count - 2, count - 1):
        finish(r)
    for copy in started:
        copy.wait_send()


def output(a, w_out, wo, emb, sizes):
    rows, depth = a.shape
    cols = emb.shape[1]
    chunks = len(sizes)
    vmem = pl.BlockSpec(memory_space=pltpu.VMEM)
    hbm = pl.BlockSpec(memory_space=pl.ANY)
    dma = pltpu.SemaphoreType.DMA
    return pl.pallas_call(
        functools.partial(output_kernel, sizes=sizes),
        out_shape=jax.ShapeDtypeStruct((rows, cols), jnp.bfloat16),
        in_specs=[hbm, hbm, hbm, vmem],
        out_specs=vmem,
        scratch_shapes=[
            pltpu.VMEM((RING, rows, depth), jnp.bfloat16),
            pltpu.VMEM((RING,) + wo.shape[:1] + wo.shape[2:], jnp.bfloat16),
            pltpu.VMEM((3, rows, cols), jnp.bfloat16),
            pltpu.VMEM((3, rows, cols), jnp.bfloat16),
            pltpu.VMEM((rows, cols), jnp.float32),
            pltpu.VMEM((rows, cols), jnp.float32),
            dma,
            dma((RING,)),
            dma((chunks, 4)),
            dma((chunks, 4)),
            dma((chunks, 6)),
            dma((chunks, 6)),
        ],
        compiler_params=pltpu.CompilerParams(
            collective_id=1, has_side_effects=True, vmem_limit_bytes=48 * MIB
        ),
        cost_estimate=pl.CostEstimate(
            flops=2 * rows * depth * RING * RING * cols, bytes_accessed=150 * MIB, transcendentals=0
        ),
        name="output",
    )(a, w_out.reshape(wo.shape[0], wo.shape[2], w_out.shape[1]), wo, emb)


def body(embedded, norm_gain, w_query, w_keyval, w_out, prefix_kv, prefix_len, needed, row_slot):
    steps, rows, width = embedded.shape
    q, own, cache, wo, begin = project(
        embedded, w_query, w_keyval, norm_gain[None], row_slot, needed, prefix_len, prefix_kv, w_out
    )
    q = q.reshape(steps, rows, q.shape[1])
    own = own.reshape(steps, rows, own.shape[1])
    attended = attend(begin, needed, prefix_len, q, own, cache, prefix_kv.shape[0])
    mixed = output(
        attended.reshape(steps * rows, width),
        w_out,
        wo,
        embedded.reshape(steps * rows, width),
        (128,) * (steps * rows // 128),
    )
    return mixed.reshape(steps, rows, width)


def solution(mesh):
    in_specs = (
        P(None, "grp", "tp"),
        P(),
        P(None, "tp"),
        P(None, "tp"),
        P("tp", None),
        P("grp", None, "tp"),
        P(),
        P(),
        P("grp", None),
    )
    out_specs = P(None, "grp", "tp")
    return jax.shard_map(body, mesh=mesh, in_specs=in_specs, out_specs=out_specs, check_vma=False)
```
